32 devices in a mesh: section: 2 (over core), dp: 16 (over z, y, x).
Axes of the slice: x: 2, y: 2, z: 4, core: 2. Of those that a mesh axis runs over, the one named last changes fastest.
Arguments:
- source: bfloat16 [2, 4096, 1024], P(None, 'dp'), may hold values from -6 to 6
- target: bfloat16 [2, 2048, 1024], P(None, 'dp'), may hold values from -6 to 6
- cotangent: bfloat16 [2, 2048, 1024], P(None, 'dp'), may hold values from -6 to 6
- source_lengths: int32 [2, 16], P(None, 'dp'), may hold values from 64 to 256, as said below
- target_lengths: int32 [2, 16], P(None, 'dp'), may hold values from 64 to 128, as said below
- attention_in: bfloat16 [2, 1024, 3072], P('section'), may hold values from -0.1875 to 0.1875
- attention_out: bfloat16 [2, 1024, 1024], P('section'), may hold values from -2 to 2
- cross_query: bfloat16 [1024, 1024], replicated, may hold values from -0.1875 to 0.1875
- cross_pair: bfloat16 [1024, 2048], replicated, may hold values from -0.1875 to 0.1875
- cross_output: bfloat16 [1024, 1024], replicated, may hold values from -2 to 2
- feed_in: bfloat16 [2, 1024, 4096], P('section'), may hold values from -0.1875 to 0.1875
- feed_out: bfloat16 [2, 4096, 1024], P('section'), may hold values from -0.09375 to 0.09375
- adapter_in: bfloat16 [2, 1024, 512], P('section'), may hold values from -0.1875 to 0.1875
- adapter_in_bias: bfloat16 [2, 512], P('section'), may hold values from -3 to 3
- adapter_out: bfloat16 [2, 512, 1024], P('section'), may hold values from -0.0625 to 0.0625
- adapter_out_bias: bfloat16 [2, 1024], P('section'), may hold values from -1.1953125 to 1.1953125
- prefix: bfloat16 [2, 2, 30, 1024], P('section'), may hold values from -6 to 6
- norm_gains: bfloat16 [2, 3, 1024], P('section'), may hold values from 0.099609375 to 1.8984375
Outputs:
- token_results: bfloat16 [2, 2, 4096, 1024], P('section', None, 'dp')
- prefix_grad: float32 [2, 2, 30, 1024], P('section')
- adapter_in_grad: float32 [2, 1024, 512], P('section', 'dp')
- adapter_out_grad: float32 [2, 512, 1024], P('section', 'dp')
- adapter_in_bias_grad: float32 [2, 512], P('section')
- adapter_out_bias_grad: float32 [2, 1024], P('section')
The draws below stay inside these ranges and needn't reach their ends.
Inputs may be any that keep to these rules, and one draw needn't show every extreme that they name: `source_lengths`: in every micro-batch at least one pair's source fills all 256 rows. `target_lengths`: in every micro-batch at least one pair's target fills all 128 rows.
All inputs are finite; a program needn't handle non-finite values.
Results may differ from the reference program's by a relative error of at most 0.019.
Values may be sent and summed in bfloat16 or wider, within the bound.
A program may use at most 192 MiB of HBM per device.

```python
import math
import jax
import jax.numpy as jnp
from jax import lax

D = 1024
HEADS = 16
HEAD_DIM = 64
FF = 4096
ADAPT = 512
PREFIX = 30
MICRO = 2
TGT_DEV = 128
SRC_DEV = 256
PAIRS = 16
SOURCES = 4096
TARGETS = 2048


def draw_source_lengths(key, part):
    key = jax.random.fold_in(key, 17)
    length_key, column_key = jax.random.split(key)
    drawn_lengths = jax.random.randint(length_key, (MICRO, PAIRS), SRC_DEV // 4, SRC_DEV + 1)
    full_column = jax.random.randint(column_key, (MICRO, 1), 0, PAIRS)
    columns = jnp.arange(PAIRS)[None, :]
    return jnp.where(columns == full_column, SRC_DEV, drawn_lengths).astype(jnp.int32)


def draw_target_lengths(key, part):
    key = jax.random.fold_in(key, 29)
    length_key, column_key = jax.random.split(key)
    drawn_lengths = jax.random.randint(length_key, (MICRO, PAIRS), TGT_DEV // 2, TGT_DEV + 1)
    full_column = jax.random.randint(column_key, (MICRO, 1), 0, PAIRS)
    columns = jnp.arange(PAIRS)[None, :]
    return jnp.where(columns == full_column, TGT_DEV, drawn_lengths).astype(jnp.int32)


def with_spikes(array, own_key, source, target, parts, factor):
    def block_of(position):
        return (jnp.arange(array.shape[position]) // (array.shape[position] // parts)).reshape((-1,) + (1,) * (array.ndim - 1 - position))

    first = jax.random.permutation(own_key, parts)[block_of(target)]
    other_side = (block_of(target) + parts // 2) % parts
    return jnp.where((block_of(source) == first) | (block_of(source) == other_side), factor * array, array)


def level_of(own_key, dims, pieces, low, top_value):
    def one(axis_at, blocks):
        draws = jax.random.uniform(jax.random.fold_in(jax.random.fold_in(own_key, 6), axis_at), (blocks,), jnp.float32, low / len(pieces), top_value / len(pieces))
        return jnp.repeat(jnp.exp(draws), dims[axis_at] // blocks).reshape((-1,) + (1,) * (len(dims) - axis_at - 1))

    gain = one(*pieces[0])
    for cut in pieces[1:]:
        gain = gain * one(*cut)
    return gain


def normal_values(stream_key, dims, scale, limit, cuts=(), dtype=jnp.bfloat16):
    values = scale * jax.random.normal(stream_key, dims, jnp.float32)
    if cuts:
        values = values * level_of(stream_key, dims, cuts, -0.22, 0.18)
    return jnp.clip(values, -limit, limit).astype(dtype)


def heavy_noise(own_key, dims, width, reach, shards, heavy, dtype=jnp.bfloat16):
    values = width * jax.random.normal(own_key, dims, jnp.float32)
    if shards:
        values = values * level_of(own_key, dims, shards, -0.22, 0.18)
    return jnp.clip(with_spikes(values, jax.random.fold_in(own_key, 3), *heavy), -reach, reach).astype(dtype)


def setup_inputs(seed: int = 0) -> dict:
    arg_keys = jax.random.split(jax.random.key(seed), 19)
    return {
        "source": heavy_noise(arg_keys[0], (MICRO, SOURCES, D), 1.0, 6.0, ((1, 16),), (1, 2, 16, 2.0)),
        "target": normal_values(arg_keys[1], (MICRO, TARGETS, D), 1.0, 6.0, ((1, 16),)),
        "cotangent": heavy_noise(arg_keys[2], (MICRO, TARGETS, D), 1.0, 6.0, ((1, 16),), (1, 2, 16, 2.0)),
        "source_lengths": draw_source_lengths(jax.random.fold_in(arg_keys[18], 71), 0),
        "target_lengths": draw_target_lengths(jax.random.fold_in(arg_keys[18], 71), 0),
        "attention_in": normal_values(arg_keys[5], (2, D, 3 * D), D ** -0.5, 0.1875, ((0, 2),)),
        "attention_out": normal_values(arg_keys[6], (2, D, D), (max(D // 128, 4)) ** -0.5, 2.0, ((0, 2),)),
        "cross_query": normal_values(arg_keys[7], (D, D), D ** -0.5, 0.1875),
        "cross_pair": normal_values(arg_keys[8], (D, 2 * D), D ** -0.5, 0.1875),
        "cross_output": normal_values(arg_keys[9], (D, D), (max(D // 128, 4)) ** -0.5, 2.0),
        "feed_in": normal_values(arg_keys[10], (2, D, FF), D ** -0.5, 0.1875, ((0, 2),)),
        "feed_out": normal_values(arg_keys[11], (2, FF, D), FF ** -0.5, 0.09375, ((0, 2),)),
        "adapter_in": normal_values(arg_keys[12], (2, D, ADAPT), D ** -0.5, 0.1875, ((0, 2),)),
        "adapter_in_bias": normal_values(arg_keys[13], (2, ADAPT), 0.5, 3.0, ((0, 2),)),
        "adapter_out": normal_values(arg_keys[14], (2, ADAPT, D), (16 * ADAPT) ** -0.5, 0.0625, ((0, 2),)),
        "adapter_out_bias": normal_values(arg_keys[15], (2, D), 0.2, 1.1953125, ((0, 2),)),
        "prefix": normal_values(arg_keys[16], (2, 2, PREFIX, D), 1.0, 6.0, ((0, 2),)),
        "norm_gains": jnp.clip(1.0 + 0.18 * jax.random.normal(arg_keys[17], (2, 3, D), jnp.float32), 0.099609375, 1.8984375).astype(jnp.bfloat16),
    }


EPS = 1e-05
NEG = -1e+30
ADAPTER_SCALE = 4.0
ROOT_HALF = 0.7071067811865476
HIGHEST_PRECISION = lax.Precision.HIGHEST

@jax.custom_vjp
def low(v):
    return lax.optimization_barrier(v.astype(jnp.bfloat16)).astype(jnp.float32)

@jax.custom_vjp
def low_back(v):
    return v

def low_keep(v):
    return (low(v), None)

def low_pass(kept, grad):
    return (grad,)

def back_keep(v):
    return (v, None)

def back_low(kept, grad):
    return (low(grad),)
low.defvjp(low_keep, low_pass)
low_back.defvjp(back_keep, back_low)

def dense_product(left, right):
    return jnp.dot(left, right, precision=HIGHEST_PRECISION)

def rounded_both(value):
    return low(low_back(value))

def smooth(value):
    return 0.5 * value * (1.0 + lax.erf(value * ROOT_HALF))

def normalize(total, norm_gain):
    centre = total - lax.optimization_barrier(jnp.mean(total, axis=-1, keepdims=True))
    return centre * lax.rsqrt(lax.optimization_barrier(jnp.mean(centre * centre, axis=-1, keepdims=True)) + EPS) * norm_gain

def split_heads(matrix):
    return matrix.reshape(matrix.shape[0], HEADS, HEAD_DIM)

def attend(queries, key_rows, value_rows, visible):
    scores = jnp.einsum('nhe,mhe->hnm', split_heads(queries), split_heads(key_rows), precision=HIGHEST_PRECISION)
    scores = low_back(scores * (1.0 / math.sqrt(HEAD_DIM)))
    scores = jnp.where(visible[None], scores, NEG)
    exponent = jnp.exp(scores - lax.optimization_barrier(jnp.max(scores, axis=-1, keepdims=True)))
    weights_low = low(exponent / lax.optimization_barrier(jnp.sum(exponent, axis=-1, keepdims=True)))
    mixed_rows = jnp.einsum('hnm,mhe->nhe', weights_low, split_heads(value_rows), precision=HIGHEST_PRECISION)
    return rounded_both(mixed_rows.reshape(queries.shape))

def self_block(rows_in, weight_in, weight_out, prefix_pair, visible, norm_gain):
    features = rows_in.shape[1]
    projected = rounded_both(dense_product(rows_in, weight_in))
    key_rows = jnp.concatenate([prefix_pair[0], projected[:, features:2 * features]], axis=0)
    value_rows = jnp.concatenate([prefix_pair[1], projected[:, 2 * features:]], axis=0)
    mixed_rows = attend(projected[:, :features], key_rows, value_rows, visible)
    return normalize(rows_in + low_back(dense_product(mixed_rows, weight_out)), norm_gain)

def branch(normed, layer_index, train, frozen, norm_gain):
    low_rows = low(normed)
    hidden = low(smooth(low_back(dense_product(low_rows, frozen[5][layer_index]))))
    feed_part = low_back(dense_product(hidden, frozen[6][layer_index]))
    bottle = low(smooth(low_back(dense_product(low_rows, train[1][layer_index]) + train[2][layer_index])))
    adapted = low_back(dense_product(bottle, train[3][layer_index]) + train[4][layer_index])
    return normalize(normed + feed_part + ADAPTER_SCALE * adapted, norm_gain)

def encode(source_rows, source_count, train, frozen):
    row_count = source_rows.shape[0]
    own_keys = jnp.broadcast_to(jnp.arange(row_count)[None, :] < source_count, (row_count, row_count))
    visible = jnp.concatenate([jnp.ones((row_count, PREFIX), bool), own_keys], axis=1)
    first_out = self_block(source_rows, frozen[0][0], frozen[1][0], train[0][0], visible, frozen[7][0, 0])
    return rounded_both(branch(first_out, 0, train, frozen, frozen[7][0, 1]))

def decode(target_rows, memory, source_count, target_count, train, frozen):
    row_count = target_rows.shape[0]
    features = target_rows.shape[1]
    positions = jnp.arange(row_count)
    causal = positions[None, :] <= positions[:, None]
    visible = jnp.concatenate([jnp.ones((row_count, PREFIX), bool), causal], axis=1)
    first_out = self_block(target_rows, frozen[0][1], frozen[1][1], train[0][1], visible, frozen[7][1, 0])
    cross_queries = rounded_both(dense_product(low(first_out), frozen[2]))
    pair_rows = rounded_both(dense_product(memory, frozen[3]))
    source_span = memory.shape[0]
    cross_visible = jnp.broadcast_to(jnp.arange(source_span)[None, :] < source_count, (row_count, source_span))
    mixed_rows = attend(cross_queries, pair_rows[:, :features], pair_rows[:, features:], cross_visible)
    second_out = normalize(first_out + low_back(dense_product(mixed_rows, frozen[4])), frozen[7][1, 1])
    third_out = branch(second_out, 1, train, frozen, frozen[7][1, 2])
    row_mask = (positions < target_count).astype(jnp.float32)[:, None]
    return third_out * row_mask

def widen(value):
    return value.astype(jnp.float32)

def reference(source, target, cotangent, source_lengths, target_lengths, attention_in, attention_out, cross_query, cross_pair, cross_output, feed_in, feed_out, adapter_in, adapter_in_bias, adapter_out, adapter_out_bias, prefix, norm_gains):
    frozen = tuple((widen(item) for item in (attention_in, attention_out, cross_query, cross_pair, cross_output, feed_in, feed_out, norm_gains)))
    train = tuple((widen(item) for item in (prefix, adapter_in, adapter_in_bias, adapter_out, adapter_out_bias)))
    block_count = MICRO * PAIRS
    source_blocks = widen(source).reshape(block_count, SRC_DEV, D)
    target_blocks = widen(target).reshape(block_count, TGT_DEV, D)
    source_counts = source_lengths.reshape(block_count)
    target_counts = target_lengths.reshape(block_count)

    def forward(train_now, source_now, target_now):

        def one_pair(item):
            source_rows, target_rows, source_count, target_count = item
            memory = encode(source_rows, source_count, train_now, frozen)
            return decode(target_rows, memory, source_count, target_count, train_now, frozen)
        return lax.map(jax.checkpoint(one_pair), (source_now, target_now, source_counts, target_counts))
    decoded, pullback = jax.vjp(forward, train, source_blocks, target_blocks)
    train_grad, source_grad, target_grad = pullback(widen(cotangent).reshape(block_count, TGT_DEV, D))
    decoded_rows = decoded.astype(jnp.bfloat16).reshape(MICRO, PAIRS, TGT_DEV, D)
    target_rows = target_grad.astype(jnp.bfloat16).reshape(MICRO, PAIRS, TGT_DEV, D)
    second_half = jnp.concatenate([decoded_rows, target_rows], axis=2).reshape(MICRO, SOURCES, D)
    first_half = source_grad.astype(jnp.bfloat16).reshape(MICRO, SOURCES, D)
    token_results = jnp.stack([first_half, second_half])
    return (token_results, train_grad[0], train_grad[1], train_grad[3], train_grad[2], train_grad[4])
```

```python
import math

import jax
import jax.numpy as jnp
from jax import lax
from jax.experimental import pallas as pl
from jax.experimental.pallas import tpu as pltpu
from jax.sharding import PartitionSpec as P

BF = jnp.bfloat16
F32 = jnp.float32
MESH = pl.DeviceIdType.MESH
EPS = 1e-05
NEG = -1e30
ROOT_HALF = 0.7071067811865476
INV_ROOT_TWO_PI = 0.3989422804014327
PRE = 30
PRE_PAD = 32
PAIR = 128
HALF = 64
LN_ROWS = 64


def dot(a, b):
    return jnp.dot(a, b, preferred_element_type=F32)


def dot_t(a, b):
    return lax.dot_general(a, b, (((1,), (1,)), ((), ())), preferred_element_type=F32)


def tdot(a, b):
    return lax.dot_general(a, b, (((0,), (0,)), ((), ())), preferred_element_type=F32)


def gelu_and_slope(v):
    cdf = 0.5 + 0.5 * lax.erf(v * ROOT_HALF)
    return v * cdf, cdf + v * (jnp.exp(-0.5 * v * v) * INV_ROOT_TWO_PI)


def rows_of(start, count):
    return pl.ds(pl.multiple_of(start, count), count)


def by_rows(count, body):
    def step(i, carry):
        body(rows_of(i * LN_ROWS, LN_ROWS))
        return carry

    lax.fori_loop(0, count // LN_ROWS, step, 0)


def norm_of(total):
    centre = total - jnp.mean(total, axis=-1, keepdims=True)
    factor = lax.rsqrt(jnp.mean(centre * centre, axis=-1, keepdims=True) + EPS)
    return centre * factor, factor


def norm_back(grad, shaped, factor, gain):
    scaled = grad * gain
    centred = scaled - jnp.mean(scaled, axis=-1, keepdims=True)
    return factor * (centred - shaped * jnp.mean(scaled * shaped, axis=-1, keepdims=True))


def both_heads(block):
    first = lax.broadcasted_iota(jnp.int32, block.shape, 1) < HALF
    zero = jnp.zeros_like(block)
    return jnp.concatenate([jnp.where(first, block, zero), jnp.where(first, zero, block)], axis=0)


def attend(rows, tokens, prefixed, pairs, q, k, vt, vtp, probs, bias, out_t):
    def step(p, carry):
        lanes = rows_of(p * PAIR, PAIR)
        scores = dot_t(k[:, lanes], both_heads(q[:, lanes]))
        shift = bias[...]
        scores = scores + jnp.concatenate([shift] * (2 * rows // PAIR), axis=1)
        power = jnp.exp(scores - jnp.max(scores, axis=0, keepdims=True))
        low = (power * (1.0 / jnp.sum(power, axis=0, keepdims=True))).astype(BF)
        probs(p)[...] = low
        for a in range(2):
            head = rows_of(p * PAIR + a * HALF, HALF)
            part = low[:, a * rows : (a + 1) * rows]
            mixed = dot(vt[head, :], part[:tokens])
            if prefixed:
                mixed = mixed + dot(vtp[head, :], part[tokens:])
            out_t[head, :] = mixed.astype(BF)
        return carry

    lax.fori_loop(0, pairs, step, 0)


def attend_back(rows, tokens, prefixed, pairs, grad, q, k, v, kt, ktp, probs, dq_t, dk, dv, pre_sum):
    def step(p, carry):
        lanes = rows_of(p * PAIR, PAIR)
        grads = both_heads(grad[:, lanes])
        queries = both_heads(q[:, lanes])
        low = probs(p)[...]
        wide = low.astype(F32)
        grad_probs = dot_t(v[:, lanes], grads)
        inner = jnp.sum(wide * grad_probs, axis=0, keepdims=True)
        grad_scores = (wide * (grad_probs - inner)).astype(BF)
        grad_keys = dot(grad_scores, queries)
        grad_values = dot(low, grads)
        dk[:, lanes] = grad_keys[:tokens].astype(BF)
        dv[:, lanes] = grad_values[:tokens].astype(BF)
        if prefixed:
            pre_sum[0, :, lanes] = pre_sum[0, :, lanes] + grad_keys[tokens:]
            pre_sum[1, :, lanes] = pre_sum[1, :, lanes] + grad_values[tokens:]
        for a in range(2):
            head = rows_of(p * PAIR + a * HALF, HALF)
            part = grad_scores[:, a * rows : (a + 1) * rows]
            back = dot(kt[head, :], part[:tokens])
            if prefixed:
                back = back + dot(ktp[head, :], part[tokens:])
            dq_t[head, :] = (back * 0.125).astype(BF)
        return carry

    lax.fori_loop(0, pairs, step, 0)


def make_kernel(nz, ny, nx, features, hidden, adapt, src_rows, tgt_rows):
    chunks = hidden // features
    pairs = features // PAIR
    dp = nz * ny * nx
    ra = features // dp
    enc_keys = src_rows + PRE_PAD
    dec_keys = tgt_rows + PRE_PAD
    small_rows = 80

    def kernel(
        src, tgt, ct, sl, tl, ai, ao, cq, cp, co, fi, fo, di, do, bi, bo, prefix, gains,
        tok, pre_out, ig_out, og_out, ib_out, ob_out,
        w, wdi, wdo, pw, k, v, kt, tt, ot, ktp, vtp, xh1, xh2, r1, r2, sa, rb, dz, snd, rcv,
        f1, dqkv, rsx, rsy, rsz, rsa, rsb, rsc, pre_sum, bias, ib_sum, ob_sum, small, small_in, small_z,
        dslope, dq_, dqc_, dxin, dct, da, kc, vc, kct,
        wsem, xsem, osem, ssem, rsem, gss, grs, mss, mrs,
    ):
        section = lax.axis_index("section")
        here = lax.axis_index("dp")
        at = {"x": lax.rem(here, nx), "y": lax.rem(here // nx, ny), "z": here // (nx * ny)}
        size = {"x": nx, "y": ny, "z": nz}

        def peer(axis, step):
            c = dict(at)
            c[axis] = lax.rem(at[axis] + step, size[axis])
            return c[axis], (section, (c["z"] * ny + c["y"]) * nx + c["x"])

        other = (1 - section, here)
        barrier = pltpu.get_barrier_semaphore()
        partners = [other] + [peer(a, s)[1] for a in "xyz" for s in range(1, size[a])]
        for partner in partners:
            pl.semaphore_signal(barrier, inc=1, device_id=partner, device_id_type=MESH)
        pl.semaphore_wait(barrier, len(partners))

        def remote(source, target, send, receive, device):
            return pltpu.make_async_remote_copy(
                src_ref=source, dst_ref=target, send_sem=send, recv_sem=receive,
                device_id=device, device_id_type=MESH,
            )

        def cross_copy(m):
            return remote(snd.at[m], rcv.at[m], ssem.at[m], rsem.at[m], other)

        widths = {"x": nx, "y": ny, "z": nz}
        orders = {"A": "xyz", "B": "yxz"}
        landing = {"A": (rsx, rsy, rsz), "B": (rsa, rsb, rsc)}

        def reduce_phase(part, stage, g):
            axis = orders[part][stage]
            count = ra
            for later in orders[part][stage + 1 :]:
                count *= size[later]
            lanes = slice(0, adapt) if part == "A" else slice(adapt, 2 * adapt)
            copies = []
            base = 0 if part == "A" else 9
            for s in range(1, size[axis]):
                c, device = peer(axis, s)
                rows = rows_of(c * count, count)
                source = g.at[rows, lanes] if stage == 0 else landing[part][stage - 1].at[0, rows]
                i = base + 3 * stage + s - 1
                copies.append(remote(source, landing[part][stage].at[s - 1], gss.at[i], grs.at[i], device))
            return copies

        def reduce_sum(part, stage, g):
            axis = orders[part][stage]
            count = ra
            for later in orders[part][stage + 1 :]:
                count *= size[later]
            lanes = slice(0, adapt) if part == "A" else slice(adapt, 2 * adapt)
            rows = rows_of(at[axis] * count, count)
            mine = g[rows, lanes] if stage == 0 else landing[part][stage - 1][0, rows]
            total = mine.astype(F32)
            for s in range(size[axis] - 1):
                total = total + landing[part][stage][s].astype(F32)
            return total

        def place(d, part):
            z, y, x = d // (nx * ny), (d // nx) % ny, d % nx
            if part == "A":
                return ((x * ny + y) * nz + z) * ra
            return ((y * nx + x) * nz + z) * ra

        def write_grads(g, ybs, dfs, count):
            first = tdot(ybs, dz[:count])
            for d in range(dp):
                g[pl.ds(place(d, "A"), ra), 0:adapt] = first[d * ra : (d + 1) * ra].astype(BF)
            second = 4.0 * tdot(rb[:count], dfs)
            half = ra // 2
            for d in range(dp):
                block = second[d * half : (d + 1) * half].astype(BF)
                g[pl.ds(place(d, "B"), half), adapt : 2 * adapt] = block[:, :adapt]
                g[pl.ds(place(d, "B") + half, half), adapt : 2 * adapt] = block[:, adapt:]

        def all_start(g, stage):
            for part in "AB":
                for c in reduce_phase(part, stage, g):
                    c.start()

        def all_finish(g, stage):
            for part in "AB":
                for c in reduce_phase(part, stage, g):
                    c.wait()
                total = reduce_sum(part, stage, g)
                if stage < 2:
                    landing[part][stage][0] = total.astype(BF)
                elif part == "A":
                    ig_out[0] = total
                else:
                    half = ra // 2
                    og_out[0, :, 0:adapt] = total[:half]
                    og_out[0, :, adapt : 2 * adapt] = total[half:]

        def small_copies(axis):
            i = {"x": 0, "y": nx - 1, "z": nx + ny - 2}[axis]
            return [
                remote(small, small_in.at[i + s - 1], mss.at[i + s - 1], mrs.at[i + s - 1], peer(axis, s)[1])
                for s in range(1, size[axis])
            ]

        def small_begin():
            small[...] = jnp.zeros_like(small)
            small[0:PRE_PAD] = pre_sum[0].astype(BF)
            small[PRE_PAD : 2 * PRE_PAD] = pre_sum[1].astype(BF)
            small[2 * PRE_PAD : 2 * PRE_PAD + 1] = ob_sum[...].astype(BF)
            small[2 * PRE_PAD + 1 : 2 * PRE_PAD + 2, 0:adapt] = ib_sum[...].astype(BF)
            small_z[...] = small[...].astype(F32)

        def small_exchange(axis):
            for c in small_copies(axis):
                c.start()
            for c in small_copies(axis):
                c.wait()
            i = {"x": 0, "y": nx - 1, "z": nx + ny - 2}[axis]
            total = small_z[...]
            for s in range(size[axis] - 1):
                total = total + small_in[i + s].astype(F32)
            small_z[...] = total
            if axis != "z":
                small[...] = total.astype(BF)

        def small_end():
            pre_out[0, 0] = small_z[0:PRE]
            pre_out[0, 1] = small_z[PRE_PAD : PRE_PAD + PRE]
            ob_out[...] = small_z[2 * PRE_PAD : 2 * PRE_PAD + 1]
            ib_out[...] = small_z[2 * PRE_PAD + 1 : 2 * PRE_PAD + 2, 0:adapt]

        blocks = {}
        for b in range(3):
            blocks[b] = (ai.at[0, :, pl.ds(b * features, features)], w.at[b])
        blocks[3] = (ao.at[0], w.at[3])
        for c in range(chunks):
            blocks[4 + c] = (fi.at[0, :, pl.ds(c * features, features)], w.at[4 + c])
            blocks[8 + c] = (fo.at[0, pl.ds(c * features, features), :], w.at[8 + c])
        blocks[12] = (cq, w.at[12])
        blocks[13] = (cp.at[:, pl.ds(0, features)], w.at[13])
        blocks[14] = (cp.at[:, pl.ds(features, features)], w.at[14])
        blocks[15] = (co, w.at[15])
        blocks[16] = (di.at[0], wdi)
        blocks[17] = (do.at[0], wdo)

        def fetch(b):
            return pltpu.make_async_copy(blocks[b][0], blocks[b][1], wsem.at[b])

        def gain(i):
            return gains[0, i : i + 1, :].astype(F32)

        def prefix_setup(tokens):
            pad = jnp.zeros((PRE_PAD, features), BF)
            for m in range(2):
                k[m, pl.ds(tokens, PRE_PAD)] = pad
                v[m, pl.ds(tokens, PRE_PAD)] = pad
                k[m, pl.ds(tokens, PRE)] = prefix[0, 0]
                v[m, pl.ds(tokens, PRE)] = prefix[0, 1]
            ktp[...] = k[0, pl.ds(tokens, PRE_PAD)].T
            vtp[...] = v[0, pl.ds(tokens, PRE_PAD)].T
            pre_sum[...] = jnp.zeros_like(pre_sum)
            ib_sum[...] = jnp.zeros_like(ib_sum)
            ob_sum[...] = jnp.zeros_like(ob_sum)

        def project(rows, x, q, m):
            q[...] = (dot(x[...], w[0]) * 0.125).astype(BF)
            keys = dot(x[...], w[1]).astype(BF)
            k[m, 0:rows] = keys
            kt[m, :, 0:rows] = keys.T
            values = dot(x[...], w[2]).astype(BF)
            v[m, 0:rows] = values
            tt[:, 0:rows] = values.T

        def branch(rows, yb, slope, m, wait):
            if wait is not None:
                wait(16)
            pre = dot(yb[...], wdi[...]) + bi[...].astype(F32)
            act, turn = gelu_and_slope(pre)
            act = act.astype(BF)
            rb[pl.ds(m * rows, rows)] = act
            sa[m, 0:rows] = turn.astype(BF)
            if wait is not None:
                wait(17)
            f1[0:rows] = f1[0:rows] + 4.0 * (dot(act, wdo[...]) + bo[...].astype(F32))

            def step(c, carry):
                if wait is not None:
                    wait(4 + c)
                act, turn = gelu_and_slope(dot(yb[...], w[4 + c]))
                slope(c)[...] = turn.astype(BF)
                if wait is not None:
                    wait(8 + c)
                f1[0:rows] = f1[0:rows] + dot(act.astype(BF), w[8 + c])
                return carry

            if wait is not None:
                for c in range(chunks):
                    step(c, 0)
            else:
                lax.fori_loop(0, chunks, step, 0)

        def branch_back(rows, df, slope, m):
            low = df[...]
            ob_sum[...] = ob_sum[...] + 4.0 * jnp.sum(low.astype(F32), axis=0, keepdims=True)
            grad = ((4.0 * dot_t(low, wdo[...])) * sa[m, 0:rows].astype(F32)).astype(BF)
            dz[pl.ds(m * rows, rows)] = grad
            ib_sum[...] = ib_sum[...] + jnp.sum(grad.astype(F32), axis=0, keepdims=True)
            f1[0:rows] = f1[0:rows] + dot_t(grad, wdi[...])

            def step(c, carry):
                grad = (dot_t(df[...], w[8 + c]) * slope(c)[...].astype(F32)).astype(BF)
                f1[0:rows] = f1[0:rows] + dot_t(grad, w[4 + c])
                return carry

            lax.fori_loop(0, chunks, step, 0)

        def self_back(rows, m, q, out):
            def norm(r):
                dt = norm_back(f1[r], xh1[m, r].astype(F32), r1[m, r], gain(0))
                f1[r] = dt
                dqkv[0, r] = dt.astype(BF)

            by_rows(rows, norm)
            ot_rows = dot_t(dqkv[0, 0:rows], w[3]).astype(BF)
            dqkv[0, 0:rows] = ot_rows
            attend_back(
                rows, rows, True, pairs, dqkv.at[0, pl.ds(0, rows)], q,
                k.at[m, pl.ds(0, rows + PRE_PAD)], v.at[m, pl.ds(0, rows + PRE_PAD)],
                kt.at[m, :, pl.ds(0, rows)], ktp,
                lambda p: pw.at[m, p, pl.ds(0, rows + PRE_PAD), pl.ds(0, 2 * rows)],
                ot.at[:, pl.ds(0, rows)], dqkv.at[1, pl.ds(0, rows)], dqkv.at[2, pl.ds(0, rows)], pre_sum,
            )
            dqkv[0, 0:rows] = ot[:, 0:rows].T
            total = f1[0:rows]
            for b in range(3):
                total = total + dot_t(dqkv[b, 0:rows], w[b])
            out[...] = total.astype(BF)

        def encoder():
            R = src_rows

            def xin(m):
                return w.at[15, pl.ds(512 + m * R, R)]

            def q(m):
                return w.at[15, pl.ds(m * R, R)]

            def yb(m):
                return w.at[14, pl.ds(m * R, R)]

            def df(m):
                return w.at[14, pl.ds(512 + m * R, R)]

            def slope(m):
                return lambda c: w.at[12 + m, rows_of(c * R, R)]

            def load_x(m):
                return pltpu.make_async_copy(src.at[m], xin(m), xsem.at[m])

            load_x(0).start()
            order = [0, 1, 2, 3, 16, 17, 4, 8, 5, 9, 6, 10, 7, 11]
            for b in order:
                fetch(b).start()
            load_x(1).start()
            prefix_setup(R)

            def forward(m):
                wait = (lambda b: fetch(b).wait()) if m == 0 else None
                load_x(m).wait()
                if wait is not None:
                    for b in range(3):
                        wait(b)
                project(R, xin(m), q(m), m)
                key = lax.broadcasted_iota(jnp.int32, (enc_keys, PAIR), 0)
                seen = (key < sl[m, 0]) | ((key >= R) & (key < R + PRE))
                bias[...] = jnp.where(seen, 0.0, NEG)
                attend(
                    R, R, True, pairs, q(m), k.at[m], tt, vtp, lambda p: pw.at[m, p], bias, ot,
                )
                if wait is not None:
                    wait(3)
                f1[...] = xin(m)[...].astype(F32) + dot(ot[...].T, w[3])

                def norm(r):
                    shaped, factor = norm_of(f1[r])
                    xh1[m, r] = shaped.astype(BF)
                    r1[m, r] = factor
                    h = shaped * gain(0)
                    f1[r] = h
                    yb(m)[r] = h.astype(BF)

                by_rows(R, norm)
                branch(R, yb(m), slope(m), m, wait)

                def last(r):
                    shaped, factor = norm_of(f1[r])
                    xh2[m, r] = shaped.astype(BF)
                    r2[m, r] = factor
                    snd[m, r] = (shaped * gain(1)).astype(BF)

                by_rows(R, last)
                cross_copy(m).start()

            def backward(m):
                cross_copy(m).wait()

                def norm(r):
                    dt = norm_back(rcv[m, r].astype(F32), xh2[m, r].astype(F32), r2[m, r], gain(1))
                    f1[r] = dt
                    df(m)[r] = dt.astype(BF)

                by_rows(R, norm)
                branch_back(R, df(m), slope(m), m)
                self_back(R, m, q(m), xin(m))
                store_x(m).start()

            def store_x(m):
                return pltpu.make_async_copy(xin(m), tok.at[0, m], osem.at[m])

            forward(0)
            forward(1)
            backward(0)
            backward(1)
            g = w.at[12]
            write_grads(g, w[14, 0 : 2 * R], w[14, 512 : 512 + 2 * R], 2 * R)
            store_x(0).wait()
            store_x(1).wait()
            reduce_all(g)

        def decoder():
            R = tgt_rows

            def shifted(r):
                return pl.ds(pl.multiple_of(r.start + R, LN_ROWS), LN_ROWS)

            def load_t(m):
                return pltpu.make_async_copy(tgt.at[m], dxin.at[m], xsem.at[m])

            def load_c(m):
                return pltpu.make_async_copy(ct.at[m], dct.at[m], xsem.at[2 + m])

            load_t(0).start()
            for b in [0, 1, 2]:
                fetch(b).start()
            load_t(1).start()
            for b in [3, 12, 13, 14, 15, 16, 17, 4, 8, 5, 9, 6, 10, 7, 11]:
                fetch(b).start()
            load_c(0).start()
            load_c(1).start()
            prefix_setup(R)

            def self_probs(m):
                return lambda p: pw.at[m, p, pl.ds(0, dec_keys), pl.ds(0, 2 * R)]

            def cross_probs(m):
                return lambda p: pw.at[m, p, pl.ds(0, src_rows), pl.ds(2 * R, 2 * R)]

            def self_forward(m):
                load_t(m).wait()
                if m == 0:
                    for b in range(3):
                        fetch(b).wait()
                project(R, dxin.at[m], dq_.at[m], m)
                key = lax.broadcasted_iota(jnp.int32, (dec_keys, PAIR), 0)
                query = lax.broadcasted_iota(jnp.int32, (dec_keys, PAIR), 1)
                seen = (key <= query) | ((key >= R) & (key < R + PRE))
                bias[0:dec_keys] = jnp.where(seen, 0.0, NEG)
                attend(
                    R, R, True, pairs, dq_.at[m], k.at[m, pl.ds(0, dec_keys)],
                    tt.at[:, pl.ds(0, R)], vtp, self_probs(m), bias.at[pl.ds(0, dec_keys)],
                    ot.at[:, pl.ds(0, R)],
                )
                if m == 0:
                    fetch(3).wait()
                f1[0:R] = dxin[m].astype(F32) + dot(ot[:, 0:R].T, w[3])

                def norm(r):
                    shaped, factor = norm_of(f1[r])
                    xh1[m, r] = shaped.astype(BF)
                    r1[m, r] = factor
                    h = shaped * gain(0)
                    da[m, r] = h
                    xh1[m, shifted(r)] = h.astype(BF)

                by_rows(R, norm)
                if m == 0:
                    fetch(12).wait()
                dqc_[m] = (dot(xh1[m, R : 2 * R], w[12]) * 0.125).astype(BF)

            def middle(m):
                cross_copy(m).wait_recv()
                if m == 0:
                    fetch(13).wait()
                    fetch(14).wait()
                keys = dot(rcv[m], w[13]).astype(BF)
                kc[...] = keys
                kct[...] = keys.T
                values = dot(rcv[m], w[14]).astype(BF)
                vc[...] = values
                tt[...] = values.T
                key = lax.broadcasted_iota(jnp.int32, (src_rows, PAIR), 0)
                bias[0:src_rows] = jnp.where(key < sl[m, 0], 0.0, NEG)
                attend(
                    R, src_rows, False, pairs, dqc_.at[m], kc, tt, None, cross_probs(m),
                    bias.at[pl.ds(0, src_rows)], ot.at[:, pl.ds(0, R)],
                )
                if m == 0:
                    fetch(15).wait()
                f1[0:R] = da[m] + dot(ot[:, 0:R].T, w[15])
                yb = xh1.at[m, pl.ds(R, R)]

                def norm(r):
                    shaped, factor = norm_of(f1[r])
                    xh2[m, r] = shaped.astype(BF)
                    r2[m, r] = factor
                    h = shaped * gain(1)
                    f1[r] = h
                    yb[r] = h.astype(BF)

                by_rows(R, norm)
                branch(R, yb, lambda c: dslope.at[c], m, (lambda b: fetch(b).wait()) if m == 0 else None)
                if m == 0:
                    load_c(0).wait()
                    load_c(1).wait()
                df = xh2.at[m, pl.ds(R, R)]

                def turn(r):
                    shaped, factor = norm_of(f1[r])
                    row = lax.broadcasted_iota(jnp.int32, (LN_ROWS, 1), 0) + r.start
                    on = jnp.where(row < tl[m, 0], 1.0, 0.0)
                    grad = dct[m, r].astype(F32) * on
                    dct[m, r] = (shaped * gain(2) * on).astype(BF)
                    dt = norm_back(grad, shaped, factor, gain(2))
                    f1[r] = dt
                    df[r] = dt.astype(BF)

                by_rows(R, turn)
                store_d(m).start()
                branch_back(R, df, lambda c: dslope.at[c], m)

                def back(r):
                    dt = norm_back(f1[r], xh2[m, r].astype(F32), r2[m, r], gain(1))
                    f1[r] = dt
                    dqkv[0, r] = dt.astype(BF)

                by_rows(R, back)
                grad_mixed = dot_t(dqkv[0, 0:R], w[15]).astype(BF)
                dqkv[0, 0:R] = grad_mixed
                attend_back(
                    R, src_rows, False, pairs, dqkv.at[0, pl.ds(0, R)], dqc_.at[m], kc, vc, kct, None,
                    cross_probs(m), ot.at[:, pl.ds(0, R)], dqkv.at[1], dqkv.at[2], None,
                )
                snd[m] = (dot_t(dqkv[1], w[13]) + dot_t(dqkv[2], w[14])).astype(BF)
                cross_copy(m).start()
                da[m] = f1[0:R] + dot_t(ot[:, 0:R].T, w[12])

            def store_d(m):
                return pltpu.make_async_copy(dct.at[m], tok.at[0, m, pl.ds(0, R)], osem.at[m])

            def store_y(m):
                return pltpu.make_async_copy(dxin.at[m], tok.at[0, m, pl.ds(R, R)], osem.at[2 + m])

            self_forward(0)
            self_forward(1)
            middle(0)
            middle(1)
            g = w.at[8]
            write_grads(
                g, xh1[:, R : 2 * R].reshape(2 * R, features), xh2[:, R : 2 * R].reshape(2 * R, features), 2 * R
            )
            for m in range(2):
                f1[0:R] = da[m]
                self_back(R, m, dq_.at[m], dxin.at[m])
                store_y(m).start()
            for m in range(2):
                store_d(m).wait()
                store_y(m).wait()
                cross_copy(m).wait_send()
            reduce_all(g)

        def reduce_all(g):
            for stage in range(3):
                all_start(g, stage)
                all_finish(g, stage)
            small_begin()
            for axis in "xyz":
                small_exchange(axis)
            small_end()

        pl.when(section == 0)(encoder)
        pl.when(section == 1)(decoder)

    enc_rows = features
    vm = pltpu.VMEM
    scratch = [
        vm((16, features, features), BF),
        vm((features, adapt), BF),
        vm((adapt, features), BF),
        vm((2, pairs, enc_keys, 2 * src_rows), BF),
        vm((2, enc_keys, features), BF),
        vm((2, enc_keys, features), BF),
        vm((2, features, src_rows), BF),
        vm((features, src_rows), BF),
        vm((features, src_rows), BF),
        vm((features, PRE_PAD), BF),
        vm((features, PRE_PAD), BF),
        vm((2, src_rows, features), BF),
        vm((2, src_rows, features), BF),
        vm((2, src_rows, 1), F32),
        vm((2, src_rows, 1), F32),
        vm((2, src_rows, adapt), BF),
        vm((2 * src_rows, adapt), BF),
        vm((2 * src_rows, adapt), BF),
        vm((2, src_rows, features), BF),
        vm((2, src_rows, features), BF),
        vm((src_rows, features), F32),
        vm((3, src_rows, features), BF),
        vm((nx - 1, ny * nz * ra, adapt), BF),
        vm((ny - 1, nz * ra, adapt), BF),
        vm((nz - 1, ra, adapt), BF),
        vm((ny - 1, nx * nz * ra, adapt), BF),
        vm((nx - 1, nz * ra, adapt), BF),
        vm((nz - 1, ra, adapt), BF),
        vm((2, PRE_PAD, features), F32),
        vm((enc_keys, PAIR), F32),
        vm((1, adapt), F32),
        vm((1, features), F32),
        vm((small_rows, features), BF),
        vm((nx + ny + nz - 3, small_rows, features), BF),
        vm((small_rows, features), F32),
        vm((chunks, tgt_rows, features), BF),
        vm((2, tgt_rows, features), BF),
        vm((2, tgt_rows, features), BF),
        vm((2, tgt_rows, features), BF),
        vm((2, tgt_rows, features), BF),
        vm((2, tgt_rows, features), F32),
        vm((src_rows, features), BF),
        vm((src_rows, features), BF),
        vm((features, src_rows), BF),
        pltpu.SemaphoreType.DMA((18,)),
        pltpu.SemaphoreType.DMA((4,)),
        pltpu.SemaphoreType.DMA((4,)),
        pltpu.SemaphoreType.DMA((2,)),
        pltpu.SemaphoreType.DMA((2,)),
        pltpu.SemaphoreType.DMA((18,)),
        pltpu.SemaphoreType.DMA((18,)),
        pltpu.SemaphoreType.DMA((9,)),
        pltpu.SemaphoreType.DMA((9,)),
    ]
    return kernel, scratch, ra


def solution(mesh):
    dp = mesh.shape["dp"]
    nz = 4
    nx = math.isqrt(dp // nz)
    ny = dp // (nz * nx)

    def per_device(
        source, target, cotangent, source_lengths, target_lengths, attention_in, attention_out,
        cross_query, cross_pair, cross_output, feed_in, feed_out, adapter_in, adapter_in_bias,
        adapter_out, adapter_out_bias, prefix, norm_gains,
    ):
        features = source.shape[2]
        adapt = adapter_in.shape[2]
        kernel, scratch, ra = make_kernel(
            nz, ny, nx, features, feed_in.shape[2], adapt, source.shape[1], target.shape[1]
        )
        anywhere = pl.BlockSpec(memory_space=pl.ANY)
        scalar = pl.BlockSpec(memory_space=pltpu.SMEM)
        vector = pl.BlockSpec(memory_space=pltpu.VMEM)
        out = pl.pallas_call(
            kernel,
            out_shape=(
                jax.ShapeDtypeStruct((1, source.shape[0], source.shape[1], features), BF),
                jax.ShapeDtypeStruct((1, 2, PRE, features), F32),
                jax.ShapeDtypeStruct((1, ra, adapt), F32),
                jax.ShapeDtypeStruct((1, ra // 2, features), F32),
                jax.ShapeDtypeStruct((1, adapt), F32),
                jax.ShapeDtypeStruct((1, features), F32),
            ),
            in_specs=[anywhere] * 3 + [scalar] * 2 + [anywhere] * 9 + [vector] * 4,
            out_specs=(anywhere, vector, vector, vector, vector, vector),
            scratch_shapes=scratch,
            compiler_params=pltpu.CompilerParams(
                collective_id=0, has_side_effects=True, vmem_limit_bytes=67000000
            ),
        )(
            source, target, cotangent, source_lengths, target_lengths, attention_in, attention_out,
            cross_query, cross_pair, cross_output, feed_in, feed_out, adapter_in, adapter_out,
            adapter_in_bias, adapter_out_bias, prefix, norm_gains,
        )
        return out

    return jax.shard_map(
        per_device,
        mesh=mesh,
        in_specs=(
            P(None, "dp", None),
            P(None, "dp", None),
            P(None, "dp", None),
            P(None, "dp"),
            P(None, "dp"),
            P("section", None, None),
            P("section", None, None),
            P(),
            P(),
            P(),
            P("section", None, None),
            P("section", None, None),
            P("section", None, None),
            P("section", None),
            P("section", None, None),
            P("section", None),
            P("section", None, None, None),
            P("section", None, None),
        ),
        out_specs=(
            P("section", None, "dp", None),
            P("section", None, None, None),
            P("section", "dp", None),
            P("section", "dp", None),
            P("section", None),
            P("section", None),
        ),
        check_vma=False,
    )
```

```python
import math

import jax
import jax.numpy as jnp
from jax import lax
from jax.experimental import pallas as pl
from jax.experimental.pallas import tpu as pltpu
from jax.sharding import PartitionSpec as P

BF = jnp.bfloat16
F32 = jnp.float32
MESH = pl.DeviceIdType.MESH
EPS = 1e-05
NEG = -1e30
ROOT_HALF = 0.7071067811865476
INV_ROOT_TWO_PI = 0.3989422804014327
PRE = 30
PRE_PAD = 32
PAIR = 128
HALF = 64
LN_ROWS = 64


def dot(a, b):
    return jnp.dot(a, b, preferred_element_type=F32)


def dot_t(a, b):
    return lax.dot_general(a, b, (((1,), (1,)), ((), ())), preferred_element_type=F32)


def tdot(a, b):
    return lax.dot_general(a, b, (((0,), (0,)), ((), ())), preferred_element_type=F32)


def gelu_and_slope(v):
    cdf = 0.5 + 0.5 * lax.erf(v * ROOT_HALF)
    return v * cdf, cdf + v * (jnp.exp(-0.5 * v * v) * INV_ROOT_TWO_PI)


def rows_of(start, count):
    return pl.ds(pl.multiple_of(start, count), count)


def by_rows(count, body):
    def step(i, carry):
        body(rows_of(i * LN_ROWS, LN_ROWS))
        return carry

    lax.fori_loop(0, count // LN_ROWS, step, 0)


def norm_of(total):
    centre = total - jnp.mean(total, axis=-1, keepdims=True)
    factor = lax.rsqrt(jnp.mean(centre * centre, axis=-1, keepdims=True) + EPS)
    return centre * factor, factor


def norm_back(grad, shaped, factor, gain):
    scaled = grad * gain
    centred = scaled - jnp.mean(scaled, axis=-1, keepdims=True)
    return factor * (centred - shaped * jnp.mean(scaled * shaped, axis=-1, keepdims=True))


def both_heads(block):
    first = lax.broadcasted_iota(jnp.int32, block.shape, 1) < HALF
    zero = jnp.zeros_like(block)
    return jnp.concatenate([jnp.where(first, block, zero), jnp.where(first, zero, block)], axis=0)


def attend(rows, tokens, prefixed, pairs, q, k, vt, vtp, probs, bias, out_t):
    def step(p, carry):
        lanes = rows_of(p * PAIR, PAIR)
        scores = dot_t(k[:, lanes], both_heads(q[:, lanes]))
        shift = bias[...]
        scores = scores + jnp.concatenate([shift] * (2 * rows // PAIR), axis=1)
        power = jnp.exp(scores - jnp.max(scores, axis=0, keepdims=True))
        low = (power * (1.0 / jnp.sum(power, axis=0, keepdims=True))).astype(BF)
        probs(p)[...] = low
        for a in range(2):
            head = rows_of(p * PAIR + a * HALF, HALF)
            part = low[:, a * rows : (a + 1) * rows]
            mixed = dot(vt[head, :], part[:tokens])
            if prefixed:
                mixed = mixed + dot(vtp[head, :], part[tokens:])
            out_t[head, :] = mixed.astype(BF)
        return carry

    lax.fori_loop(0, pairs, step, 0, unroll=4)


def attend_back(rows, tokens, prefixed, pairs, grad, q, k, v, kt, ktp, probs, dq_t, dk, dv, pre_sum):
    def step(p, carry):
        lanes = rows_of(p * PAIR, PAIR)
        grads = both_heads(grad[:, lanes])
        queries = both_heads(q[:, lanes])
        low = probs(p)[...]
        wide = low.astype(F32)
        grad_probs = dot_t(v[:, lanes], grads)
        inner = jnp.sum(wide * grad_probs, axis=0, keepdims=True)
        grad_scores = (wide * (grad_probs - inner)).astype(BF)
        grad_keys = dot(grad_scores, queries)
        grad_values = dot(low, grads)
        dk[:, lanes] = grad_keys[:tokens].astype(BF)
        dv[:, lanes] = grad_values[:tokens].astype(BF)
        if prefixed:
            pre_sum[0, :, lanes] = pre_sum[0, :, lanes] + grad_keys[tokens:]
            pre_sum[1, :, lanes] = pre_sum[1, :, lanes] + grad_values[tokens:]
        for a in range(2):
            head = rows_of(p * PAIR + a * HALF, HALF)
            part = grad_scores[:, a * rows : (a + 1) * rows]
            back = dot(kt[head, :], part[:tokens])
            if prefixed:
                back = back + dot(ktp[head, :], part[tokens:])
            dq_t[head, :] = (back * 0.125).astype(BF)
        return carry

    lax.fori_loop(0, pairs, step, 0, unroll=4)


def make_kernel(nz, ny, nx, features, hidden, adapt, src_rows, tgt_rows):
    chunks = hidden // features
    pairs = features // PAIR
    dp = nz * ny * nx
    ra = features // dp
    enc_keys = src_rows + PRE_PAD
    dec_keys = tgt_rows + PRE_PAD
    small_rows = 2 * PRE_PAD

    def kernel(
        src, tgt, ct, sl, tl, ai, ao, cq, cp, co, fi, fo, di, do, bi, bo, prefix, gains,
        tok, ig_out, og_out, sm_out,
        w, wdi, wdo, pw, k, v, kt, tt, ot, ktp, vtp, xh1, xh2, r1, r2, sa, rb, dz, snd, rcv,
        f1, dqkv, rsx, rsy, rsz, rsa, rsb, rsc, pre_sum, bias, ib_sum, ob_sum,
        small, small_in, small_mid, small_z, small_end, small_all,
        dxin, dct, da, kc, vc, kct,
        wsem, xsem, osem, ssem, rsem, gss, grs, mss, mrs,
    ):
        section = lax.axis_index("section")
        here = lax.axis_index("dp")
        at = {"x": lax.rem(here, nx), "y": lax.rem(here // nx, ny), "z": here // (nx * ny)}
        size = {"x": nx, "y": ny, "z": nz}

        def peer(axis, step):
            c = dict(at)
            c[axis] = lax.rem(at[axis] + step, size[axis])
            return c[axis], (section, (c["z"] * ny + c["y"]) * nx + c["x"])

        other = (1 - section, here)
        barrier = pltpu.get_barrier_semaphore()
        partners = [other] + [peer("z", s)[1] for s in range(1, nz)]
        for s in range(1, nx * ny):
            partners.append((section, at["z"] * nx * ny + lax.rem(at["y"] * nx + at["x"] + s, nx * ny)))
        for partner in partners:
            pl.semaphore_signal(barrier, inc=1, device_id=partner, device_id_type=MESH)
        pl.semaphore_wait(barrier, len(partners))

        def remote(source, target, send, receive, device):
            return pltpu.make_async_remote_copy(
                src_ref=source, dst_ref=target, send_sem=send, recv_sem=receive,
                device_id=device, device_id_type=MESH,
            )

        def cross_copy(m):
            return remote(snd, rcv.at[m], ssem.at[m], rsem.at[m], other)

        widths = {"x": nx, "y": ny, "z": nz}
        orders = {"A": "xyz", "B": "yxz"}
        landing = {"A": (rsx, rsy, rsz), "B": (rsa, rsb, rsc)}

        def reduce_phase(part, stage, g):
            axis = orders[part][stage]
            count = ra
            for later in orders[part][stage + 1 :]:
                count *= size[later]
            lanes = slice(0, adapt) if part == "A" else slice(adapt, 2 * adapt)
            copies = []
            base = 0 if part == "A" else 9
            for s in range(1, size[axis]):
                c, device = peer(axis, s)
                rows = rows_of(c * count, count)
                source = g.at[rows, lanes] if stage == 0 else landing[part][stage - 1].at[0, rows]
                i = base + 3 * stage + s - 1
                copies.append(remote(source, landing[part][stage].at[s - 1], gss.at[i], grs.at[i], device))
            return copies

        def reduce_sum(part, stage, g):
            axis = orders[part][stage]
            count = ra
            for later in orders[part][stage + 1 :]:
                count *= size[later]
            lanes = slice(0, adapt) if part == "A" else slice(adapt, 2 * adapt)
            rows = rows_of(at[axis] * count, count)
            mine = g[rows, lanes] if stage == 0 else landing[part][stage - 1][0, rows]
            total = mine.astype(F32)
            for s in range(size[axis] - 1):
                total = total + landing[part][stage][s].astype(F32)
            return total

        def place(d, part):
            z, y, x = d // (nx * ny), (d // nx) % ny, d % nx
            if part == "A":
                return ((x * ny + y) * nz + z) * ra
            return ((y * nx + x) * nz + z) * ra

        def write_grads(g, ybs, dfs, count):
            first = tdot(ybs, dz[:count])
            for d in range(dp):
                g[pl.ds(place(d, "A"), ra), 0:adapt] = first[d * ra : (d + 1) * ra].astype(BF)
            second = 4.0 * tdot(rb[:count], dfs)
            half = ra // 2
            for d in range(dp):
                block = second[d * half : (d + 1) * half].astype(BF)
                g[pl.ds(place(d, "B"), half), adapt : 2 * adapt] = block[:, :adapt]
                g[pl.ds(place(d, "B") + half, half), adapt : 2 * adapt] = block[:, adapt:]

        def all_start(g, stage):
            for part in "AB":
                for c in reduce_phase(part, stage, g):
                    c.start()

        def all_finish(g, stage):
            for part in "AB":
                for c in reduce_phase(part, stage, g):
                    c.wait()
                total = reduce_sum(part, stage, g)
                if stage < 2:
                    landing[part][stage][0] = total.astype(BF)
                elif part == "A":
                    ig_out[...] = total
                else:
                    half = ra // 2
                    og_out[:, 0:adapt] = total[:half]
                    og_out[:, adapt : 2 * adapt] = total[half:]

        plane = nx * ny
        piece = small_rows * features // (16 * plane)
        across = features // piece
        seat = at["y"] * nx + at["x"]

        def plane_peer(s):
            i = lax.rem(seat + s, plane)
            return i, (section, at["z"] * plane + i)

        def small_at(ref, i):
            return ref.at[rows_of((i // across) * 16, 16), rows_of(lax.rem(i, across) * piece, piece)]

        def small_scatter():
            copies = []
            for s in range(1, plane):
                i, device = plane_peer(s)
                copies.append(remote(small_at(small, i), small_in.at[s - 1], mss.at[s - 1], mrs.at[s - 1], device))
            return copies

        def small_along():
            n = plane - 1
            return [
                remote(small_mid, small_z.at[s - 1], mss.at[n + s - 1], mrs.at[n + s - 1], peer("z", s)[1])
                for s in range(1, nz)
            ]

        def small_gather():
            n = plane - 1 + nz - 1
            copies = []
            for s in range(1, plane):
                device = plane_peer(s)[1]
                copies.append(
                    remote(small_end, small_at(small_all, seat), mss.at[n + s - 1], mrs.at[n + s - 1], device)
                )
            return copies

        def small_begin():
            small[0:PRE_PAD] = pre_sum[0].astype(BF)
            small[PRE_PAD : 2 * PRE_PAD] = pre_sum[1].astype(BF)
            small[PRE : PRE + 1] = ob_sum[...].astype(BF)
            small[PRE_PAD + PRE : PRE_PAD + PRE + 1, 0:adapt] = ib_sum[...].astype(BF)
            for c in small_scatter():
                c.start()

        def small_middle():
            for c in small_scatter():
                c.wait()
            total = small_at(small, seat)[...].astype(F32)
            for s in range(plane - 1):
                total = total + small_in[s].astype(F32)
            small_mid[...] = total.astype(BF)
            for c in small_along():
                c.start()

        def small_late():
            for c in small_along():
                c.wait()
            total = small_mid[...].astype(F32)
            for s in range(nz - 1):
                total = total + small_z[s].astype(F32)
            small_end[...] = total.astype(BF)
            small_at(small_all, seat)[...] = small_end[...]
            for c in small_gather():
                c.start()

        def small_finish():
            for c in small_gather():
                c.wait()
            sm_out[...] = small_all[...].astype(F32)

        blocks = {}
        for b in range(3):
            blocks[b] = (ai.at[0, :, pl.ds(b * features, features)], w.at[b])
        blocks[3] = (ao.at[0], w.at[3])
        for c in range(chunks):
            blocks[4 + c] = (fi.at[0, :, pl.ds(c * features, features)], w.at[4 + c])
            blocks[8 + c] = (fo.at[0, pl.ds(c * features, features), :], w.at[8 + c])
        blocks[12] = (cq, w.at[12])
        blocks[13] = (cp.at[:, pl.ds(0, features)], w.at[13])
        blocks[14] = (cp.at[:, pl.ds(features, features)], w.at[14])
        blocks[15] = (co, w.at[15])
        blocks[16] = (di.at[0], wdi)
        blocks[17] = (do.at[0], wdo)

        def fetch(b):
            return pltpu.make_async_copy(blocks[b][0], blocks[b][1], wsem.at[b])

        def gain(i):
            return gains[0, i : i + 1, :].astype(F32)

        def prefix_setup(tokens):
            pad = jnp.zeros((PRE_PAD, features), BF)
            for m in range(2):
                k[m, pl.ds(tokens, PRE_PAD)] = pad
                v[m, pl.ds(tokens, PRE_PAD)] = pad
                k[m, pl.ds(tokens, PRE)] = prefix[:, 0, :]
                v[m, pl.ds(tokens, PRE)] = prefix[:, 1, :]
            ktp[...] = k[0, pl.ds(tokens, PRE_PAD)].T
            vtp[...] = v[0, pl.ds(tokens, PRE_PAD)].T
            pre_sum[...] = jnp.zeros_like(pre_sum)
            ib_sum[...] = jnp.zeros_like(ib_sum)
            ob_sum[...] = jnp.zeros_like(ob_sum)

        def project(rows, x, q, m):
            q[...] = (dot(x[...], w[0]) * 0.125).astype(BF)
            keys = dot(x[...], w[1]).astype(BF)
            k[m, 0:rows] = keys
            kt[m, :, 0:rows] = keys.T
            values = dot(x[...], w[2]).astype(BF)
            v[m, 0:rows] = values
            tt[:, 0:rows] = values.T

        def branch(rows, yb, slope, m, wait):
            if wait is not None:
                wait(16)
            pre = dot(yb[...], wdi[...]) + bi[...].astype(F32)
            act, turn = gelu_and_slope(pre)
            act = act.astype(BF)
            rb[pl.ds(m * rows, rows)] = act
            sa[m, 0:rows] = turn.astype(BF)
            if wait is not None:
                wait(17)
            f1[0:rows] = f1[0:rows] + 4.0 * (dot(act, wdo[...]) + bo[...].astype(F32))

            def step(c, carry):
                if wait is not None:
                    wait(4 + c)
                act, turn = gelu_and_slope(dot(yb[...], w[4 + c]))
                slope[1](c, turn.astype(BF))
                if wait is not None:
                    wait(8 + c)
                f1[0:rows] = f1[0:rows] + dot(act.astype(BF), w[8 + c])
                return carry

            if wait is not None:
                for c in range(chunks):
                    step(c, 0)
            else:
                lax.fori_loop(0, chunks, step, 0)

        def branch_back_adapter(rows, df, m):
            low = df[...]
            ob_sum[...] = ob_sum[...] + 4.0 * jnp.sum(low.astype(F32), axis=0, keepdims=True)
            grad = ((4.0 * dot_t(low, wdo[...])) * sa[m, 0:rows].astype(F32)).astype(BF)
            dz[pl.ds(m * rows, rows)] = grad
            ib_sum[...] = ib_sum[...] + jnp.sum(grad.astype(F32), axis=0, keepdims=True)

        def branch_back_feed(rows, df, slope, m):
            f1[0:rows] = f1[0:rows] + dot_t(dz[pl.ds(m * rows, rows)], wdi[...])

            def step(c, carry):
                grad = (dot_t(df[...], w[8 + c]) * slope[0](c).astype(F32)).astype(BF)
                f1[0:rows] = f1[0:rows] + dot_t(grad, w[4 + c])
                return carry

            lax.fori_loop(0, chunks, step, 0)

        def self_back(rows, m, q):
            def norm(r):
                dt = norm_back(f1[r], xh1[m, r].astype(F32), r1[m, r], gain(0))
                f1[r] = dt
                dqkv[0, r] = dt.astype(BF)

            by_rows(rows, norm)
            ot_rows = dot_t(dqkv[0, 0:rows], w[3]).astype(BF)
            dqkv[0, 0:rows] = ot_rows
            attend_back(
                rows, rows, True, pairs, dqkv.at[0, pl.ds(0, rows)], q,
                k.at[m, pl.ds(0, rows + PRE_PAD)], v.at[m, pl.ds(0, rows + PRE_PAD)],
                kt.at[m, :, pl.ds(0, rows)], ktp,
                lambda p: pw.at[m, p, pl.ds(0, rows + PRE_PAD), pl.ds(0, 2 * rows)],
                ot.at[:, pl.ds(0, rows)], dqkv.at[1, pl.ds(0, rows)], dqkv.at[2, pl.ds(0, rows)], pre_sum,
            )
            dqkv[0, 0:rows] = ot[:, 0:rows].T

        def self_input(rows, out):
            total = f1[0:rows]
            for b in range(3):
                total = total + dot_t(dqkv[b, 0:rows], w[b])
            out[...] = total.astype(BF)

        def encoder():
            R = src_rows

            def xin(m):
                return w.at[15, pl.ds(512 + m * R, R)]

            def q(m):
                return w.at[15, pl.ds(m * R, R)]

            def yb(m):
                return w.at[14, pl.ds(m * R, R)]

            def df(m):
                return w.at[14, pl.ds(512 + m * R, R)]

            def slope(m):
                def put(c, value):
                    w[12 + m, rows_of(c * R, R)] = value

                return (lambda c: w[12 + m, rows_of(c * R, R)]), put

            def load_x(m):
                return pltpu.make_async_copy(src.at[m], xin(m), xsem.at[m])

            load_x(0).start()
            for b in (0, 1, 2):
                fetch(b).start()
            load_x(1).start()
            prefix_setup(R)

            def forward(m):
                wait = (lambda b: fetch(b).wait()) if m == 0 else None
                load_x(m).wait()
                if wait is not None:
                    wait(0)
                    for b in (3, 16, 17, 4, 8):
                        fetch(b).start()
                    wait(1)
                    wait(2)
                    for b in (5, 9, 6, 10, 7, 11):
                        fetch(b).start()
                project(R, xin(m), q(m), m)
                key = lax.broadcasted_iota(jnp.int32, (enc_keys, PAIR), 0)
                seen = (key < sl[m]) | ((key >= R) & (key < R + PRE))
                bias[...] = jnp.where(seen, 0.0, NEG)
                attend(
                    R, R, True, pairs, q(m), k.at[m], tt, vtp, lambda p: pw.at[m, p], bias, ot,
                )
                if wait is not None:
                    wait(3)
                f1[...] = xin(m)[...].astype(F32) + dot(ot[...].T, w[3])

                def norm(r):
                    shaped, factor = norm_of(f1[r])
                    xh1[m, r] = shaped.astype(BF)
                    r1[m, r] = factor
                    h = shaped * gain(0)
                    f1[r] = h
                    yb(m)[r] = h.astype(BF)

                by_rows(R, norm)
                branch(R, yb(m), slope(m), m, wait)

                if m == 1:
                    cross_copy(0).wait_send()

                def last(r):
                    shaped, factor = norm_of(f1[r])
                    xh2[m, r] = shaped.astype(BF)
                    r2[m, r] = factor
                    snd[r] = (shaped * gain(1)).astype(BF)

                by_rows(R, last)
                cross_copy(m).start()

            def backward(m):
                if m == 0:
                    cross_copy(1).wait_send()
                cross_copy(m).wait_recv()

                def norm(r):
                    dt = norm_back(rcv[m, r].astype(F32), xh2[m, r].astype(F32), r2[m, r], gain(1))
                    f1[r] = dt
                    df(m)[r] = dt.astype(BF)

                by_rows(R, norm)
                branch_back_adapter(R, df(m), m)
                g = w.at[12]
                if m == 1:
                    write_grads(g, w[14, 0 : 2 * R], w[14, 512 : 512 + 2 * R], 2 * R)
                    all_start(g, 0)
                branch_back_feed(R, df(m), slope(m), m)
                if m == 1:
                    all_finish(g, 0)
                    all_start(g, 1)
                self_back(R, m, q(m))
                if m == 1:
                    small_begin()
                    all_finish(g, 1)
                    all_start(g, 2)
                self_input(R, xin(m))
                store_x(m).start()

            def store_x(m):
                return pltpu.make_async_copy(xin(m), tok.at[0, m], osem.at[m])

            forward(0)
            forward(1)
            backward(0)
            backward(1)
            small_middle()
            all_finish(w.at[12], 2)
            small_late()
            store_x(0).wait()
            store_x(1).wait()
            small_finish()

        def decoder():
            R = tgt_rows

            def shifted(r):
                return pl.ds(pl.multiple_of(r.start + R, LN_ROWS), LN_ROWS)

            def load_t(m):
                return pltpu.make_async_copy(tgt.at[m], dxin.at[m], xsem.at[m])

            def load_c(m):
                return pltpu.make_async_copy(ct.at[m], dct.at[m], xsem.at[2 + m])

            load_t(0).start()
            for b in [0, 1, 2]:
                fetch(b).start()
            load_t(1).start()
            for b in [3, 12, 13, 14, 15, 16, 17, 4, 8, 5, 9, 6, 10, 7, 11]:
                fetch(b).start()
            load_c(0).start()
            load_c(1).start()
            prefix_setup(R)

            def pick(c):
                parts = [pw[1, 2 * c + i // 2, pl.ds((i % 2) * R, R), 256:512] for i in range(4)]
                return jnp.concatenate(parts, axis=1)

            def put(c, value):
                for i in range(4):
                    pw[1, 2 * c + i // 2, pl.ds((i % 2) * R, R), 256:512] = value[:, 256 * i : 256 * (i + 1)]

            slope = (pick, put)

            def early(m):
                return f1.at[pl.ds(R, R)] if m == 0 else da

            def dq_(m):
                return k.at[m, pl.ds(dec_keys, R)]

            def dqc_(m):
                return v.at[m, pl.ds(dec_keys, R)]

            def self_probs(m):
                return lambda p: pw.at[m, p, pl.ds(0, dec_keys), pl.ds(0, 2 * R)]

            def cross_probs():
                return lambda p: pw.at[0, p, pl.ds(0, src_rows), pl.ds(2 * R, 2 * R)]

            def self_forward(m):
                load_t(m).wait()
                if m == 0:
                    for b in range(3):
                        fetch(b).wait()
                project(R, dxin.at[m], dq_(m), m)
                key = lax.broadcasted_iota(jnp.int32, (dec_keys, PAIR), 0)
                query = lax.broadcasted_iota(jnp.int32, (dec_keys, PAIR), 1)
                seen = (key <= query) | ((key >= R) & (key < R + PRE))
                bias[0:dec_keys] = jnp.where(seen, 0.0, NEG)
                attend(
                    R, R, True, pairs, dq_(m), k.at[m, pl.ds(0, dec_keys)],
                    tt.at[:, pl.ds(0, R)], vtp, self_probs(m), bias.at[pl.ds(0, dec_keys)],
                    ot.at[:, pl.ds(0, R)],
                )
                if m == 0:
                    fetch(3).wait()
                f1[0:R] = dxin[m].astype(F32) + dot(ot[:, 0:R].T, w[3])

                def norm(r):
                    shaped, factor = norm_of(f1[r])
                    xh1[m, r] = shaped.astype(BF)
                    r1[m, r] = factor
                    h = shaped * gain(0)
                    early(m)[r] = h
                    xh1[m, shifted(r)] = h.astype(BF)

                by_rows(R, norm)
                if m == 0:
                    fetch(12).wait()
                dqc_(m)[...] = (dot(xh1[m, R : 2 * R], w[12]) * 0.125).astype(BF)

            def middle(m):
                cross_copy(m).wait_recv()
                if m == 0:
                    fetch(13).wait()
                    fetch(14).wait()
                keys = dot(rcv[m], w[13]).astype(BF)
                kc[...] = keys
                kct[...] = keys.T
                values = dot(rcv[m], w[14]).astype(BF)
                vc[...] = values
                tt[...] = values.T
                key = lax.broadcasted_iota(jnp.int32, (src_rows, PAIR), 0)
                bias[0:src_rows] = jnp.where(key < sl[m], 0.0, NEG)
                attend(
                    R, src_rows, False, pairs, dqc_(m), kc, tt, None, cross_probs(),
                    bias.at[pl.ds(0, src_rows)], ot.at[:, pl.ds(0, R)],
                )
                if m == 0:
                    fetch(15).wait()
                f1[0:R] = early(m)[...] + dot(ot[:, 0:R].T, w[15])
                yb = xh1.at[m, pl.ds(R, R)]

                def norm(r):
                    shaped, factor = norm_of(f1[r])
                    xh2[m, r] = shaped.astype(BF)
                    r2[m, r] = factor
                    h = shaped * gain(1)
                    f1[r] = h
                    yb[r] = h.astype(BF)

                by_rows(R, norm)
                branch(R, yb, slope, m, (lambda b: fetch(b).wait()) if m == 0 else None)
                if m == 0:
                    load_c(0).wait()
                    load_c(1).wait()
                df = xh2.at[m, pl.ds(R, R)]

                def turn(r):
                    shaped, factor = norm_of(f1[r])
                    row = lax.broadcasted_iota(jnp.int32, (LN_ROWS, 1), 0) + r.start
                    on = jnp.where(row < tl[m], 1.0, 0.0)
                    grad = dct[m, r].astype(F32) * on
                    dct[m, r] = (shaped * gain(2) * on).astype(BF)
                    dt = norm_back(grad, shaped, factor, gain(2))
                    f1[r] = dt
                    df[r] = dt.astype(BF)

                by_rows(R, turn)
                store_d(m).start()
                branch_back_adapter(R, df, m)
                branch_back_feed(R, df, slope, m)
                if m == 1:
                    write_grads(
                        g, xh1[:, R : 2 * R].reshape(2 * R, features), xh2[:, R : 2 * R].reshape(2 * R, features), 2 * R
                    )
                    all_start(g, 0)

                def back(r):
                    dt = norm_back(f1[r], xh2[m, r].astype(F32), r2[m, r], gain(1))
                    f1[r] = dt
                    dqkv[0, r] = dt.astype(BF)

                by_rows(R, back)
                grad_mixed = dot_t(dqkv[0, 0:R], w[15]).astype(BF)
                dqkv[0, 0:R] = grad_mixed
                attend_back(
                    R, src_rows, False, pairs, dqkv.at[0, pl.ds(0, R)], dqc_(m), kc, vc, kct, None,
                    cross_probs(), ot.at[:, pl.ds(0, R)], dqkv.at[1], dqkv.at[2], None,
                )
                if m == 1:
                    cross_copy(0).wait_send()
                snd[...] = (dot_t(dqkv[1], w[13]) + dot_t(dqkv[2], w[14])).astype(BF)
                cross_copy(m).start()
                early(m)[...] = f1[0:R] + dot_t(ot[:, 0:R].T, w[12])

            def store_d(m):
                return pltpu.make_async_copy(dct.at[m], tok.at[0, m, pl.ds(0, R)], osem.at[m])

            def store_y(m):
                return pltpu.make_async_copy(dxin.at[m], tok.at[0, m, pl.ds(R, R)], osem.at[2 + m])

            g = w.at[8]
            self_forward(0)
            self_forward(1)
            middle(0)
            middle(1)
            all_finish(g, 0)
            all_start(g, 1)
            for m in range(2):
                f1[0:R] = early(m)[...]
                self_back(R, m, dq_(m))
                if m == 0:
                    self_input(R, dxin.at[m])
                    store_y(m).start()
                    all_finish(g, 1)
                    all_start(g, 2)
            small_begin()
            self_input(R, dxin.at[1])
            store_y(1).start()
            small_middle()
            all_finish(g, 2)
            small_late()
            for m in range(2):
                store_d(m).wait()
                store_y(m).wait()
            cross_copy(1).wait_send()
            small_finish()

        pl.when(section == 0)(encoder)
        pl.when(section == 1)(decoder)

    vm = pltpu.VMEM
    plane = nx * ny
    piece = small_rows * features // (16 * plane)
    smalls = 2 * (plane - 1) + nz - 1
    scratch = [
        vm((16, features, features), BF),
        vm((features, adapt), BF),
        vm((adapt, features), BF),
        vm((2, pairs, enc_keys, 2 * src_rows), BF),
        vm((2, enc_keys, features), BF),
        vm((2, enc_keys, features), BF),
        vm((2, features, src_rows), BF),
        vm((features, src_rows), BF),
        vm((features, src_rows), BF),
        vm((features, PRE_PAD), BF),
        vm((features, PRE_PAD), BF),
        vm((2, src_rows, features), BF),
        vm((2, src_rows, features), BF),
        vm((2, src_rows, 1), F32),
        vm((2, src_rows, 1), F32),
        vm((2, src_rows, adapt), BF),
        vm((2 * src_rows, adapt), BF),
        vm((2 * src_rows, adapt), BF),
        vm((src_rows, features), BF),
        vm((2, src_rows, features), BF),
        vm((src_rows, features), F32),
        vm((3, src_rows, features), BF),
        vm((nx - 1, ny * nz * ra, adapt), BF),
        vm((ny - 1, nz * ra, adapt), BF),
        vm((nz - 1, ra, adapt), BF),
        vm((ny - 1, nx * nz * ra, adapt), BF),
        vm((nx - 1, nz * ra, adapt), BF),
        vm((nz - 1, ra, adapt), BF),
        vm((2, PRE_PAD, features), F32),
        vm((enc_keys, PAIR), F32),
        vm((1, adapt), F32),
        vm((1, features), F32),
        vm((small_rows, features), BF),
        vm((plane - 1, 16, piece), BF),
        vm((16, piece), BF),
        vm((nz - 1, 16, piece), BF),
        vm((16, piece), BF),
        vm((small_rows, features), BF),
        vm((2, tgt_rows, features), BF),
        vm((2, tgt_rows, features), BF),
        vm((tgt_rows, features), F32),
        vm((src_rows, features), BF),
        vm((src_rows, features), BF),
        vm((features, src_rows), BF),
        pltpu.SemaphoreType.DMA((18,)),
        pltpu.SemaphoreType.DMA((4,)),
        pltpu.SemaphoreType.DMA((4,)),
        pltpu.SemaphoreType.DMA((2,)),
        pltpu.SemaphoreType.DMA((2,)),
        pltpu.SemaphoreType.DMA((18,)),
        pltpu.SemaphoreType.DMA((18,)),
        pltpu.SemaphoreType.DMA((smalls,)),
        pltpu.SemaphoreType.DMA((smalls,)),
    ]
    return kernel, scratch, ra


def finish(tok, ig, og, small, tok_out, pre_out, ig_out, og_out, ib_out, ob_out, sem):
    copy = pltpu.make_async_copy(tok, tok_out, sem)
    copy.start()
    adapt = ig.shape[1]
    pre_out[:, 0, :] = small[0:PRE]
    pre_out[:, 1, :] = small[PRE_PAD : PRE_PAD + PRE]
    ig_out[0] = ig[...]
    og_out[0] = og[...]
    ob_out[...] = small[PRE : PRE + 1]
    ib_out[...] = small[PRE_PAD + PRE : PRE_PAD + PRE + 1, 0:adapt]
    copy.wait()


def solution(mesh):
    dp = mesh.shape["dp"]
    nz = 4
    nx = math.isqrt(dp // nz)
    ny = dp // (nz * nx)

    def per_device(
        source, target, cotangent, source_lengths, target_lengths, attention_in, attention_out,
        cross_query, cross_pair, cross_output, feed_in, feed_out, adapter_in, adapter_in_bias,
        adapter_out, adapter_out_bias, prefix, norm_gains,
    ):
        features = source.shape[2]
        adapt = adapter_in.shape[2]
        kernel, scratch, ra = make_kernel(
            nz, ny, nx, features, feed_in.shape[2], adapt, source.shape[1], target.shape[1]
        )
        anywhere = pl.BlockSpec(memory_space=pl.ANY)
        scalar = pl.BlockSpec(memory_space=pltpu.SMEM)
        vector = pl.BlockSpec(memory_space=pltpu.VMEM)
        tok, ig, og, small = pl.pallas_call(
            kernel,
            out_shape=(
                jax.ShapeDtypeStruct((1, source.shape[0], source.shape[1], features), BF),
                jax.ShapeDtypeStruct((ra, adapt), F32),
                jax.ShapeDtypeStruct((ra // 2, features), F32),
                jax.ShapeDtypeStruct((2 * PRE_PAD, features), F32),
            ),
            in_specs=[anywhere] * 3 + [scalar] * 2 + [anywhere] * 9 + [vector] * 4,
            out_specs=(anywhere, vector, vector, vector),
            scratch_shapes=scratch,
            compiler_params=pltpu.CompilerParams(
                collective_id=0, has_side_effects=True, vmem_limit_bytes=67000000
            ),
        )(
            source, target, cotangent, source_lengths.reshape(-1), target_lengths.reshape(-1), attention_in,
            attention_out, cross_query, cross_pair, cross_output, feed_in, feed_out, adapter_in, adapter_out,
            adapter_in_bias, adapter_out_bias, prefix[0].transpose(1, 0, 2), norm_gains,
        )
        tok, pre, ig, og, ib, ob = pl.pallas_call(
            finish,
            out_shape=(
                jax.ShapeDtypeStruct(tok.shape, BF),
                jax.ShapeDtypeStruct((PRE, 2, features), F32),
                jax.ShapeDtypeStruct((1, ra, adapt), F32),
                jax.ShapeDtypeStruct((1, ra // 2, features), F32),
                jax.ShapeDtypeStruct((1, adapt), F32),
                jax.ShapeDtypeStruct((1, features), F32),
            ),
            in_specs=[anywhere, vector, vector, vector],
            out_specs=(vector, vector, vector, vector, vector, vector),
            scratch_shapes=[pltpu.SemaphoreType.DMA(())],
        )(tok, ig, og, small)
        return tok, pre.transpose(1, 0, 2)[None], ig, og, ib, ob

    return jax.shard_map(
        per_device,
        mesh=mesh,
        in_specs=(
            P(None, "dp", None),
            P(None, "dp", None),
            P(None, "dp", None),
            P(None, "dp"),
            P(None, "dp"),
            P("section", None, None),
            P("section", None, None),
            P(),
            P(),
            P(),
            P("section", None, None),
            P("section", None, None),
            P("section", None, None),
            P("section", None),
            P("section", None, None),
            P("section", None),
            P("section", None, None, None),
            P("section", None, None),
        ),
        out_specs=(
            P("section", None, "dp", None),
            P("section", None, None, None),
            P("section", "dp", None),
            P("section", "dp", None),
            P("section", None),
            P("section", None),
        ),
        check_vma=False,
    )
```

```python
import math

import jax
import jax.numpy as jnp
from jax import lax
from jax.experimental import pallas as pl
from jax.experimental.pallas import tpu as pltpu
from jax.sharding import PartitionSpec as P

BF = jnp.bfloat16
F32 = jnp.float32
MESH = pl.DeviceIdType.MESH
EPS = 1e-05
NEG = -1e30
ROOT_HALF = 0.7071067811865476
INV_ROOT_TWO_PI = 0.3989422804014327
PRE = 30
PRE_PAD = 32
PAIR = 128
HALF = 64
LN_ROWS = 128
ENC_PAIRS = 4
SELF_PAIRS = 2
CROSS_PAIRS = 8
ENC_CHUNKS = 1
DEC_CHUNKS = 4


def dot(a, b):
    return jnp.dot(a, b, preferred_element_type=F32)


def dot_t(a, b):
    return lax.dot_general(a, b, (((1,), (1,)), ((), ())), preferred_element_type=F32)


def tdot(a, b):
    return lax.dot_general(a, b, (((0,), (0,)), ((), ())), preferred_element_type=F32)


def gelu_and_slope(v):
    cdf = 0.5 + 0.5 * lax.erf(v * ROOT_HALF)
    return v * cdf, cdf + v * (jnp.exp(-0.5 * v * v) * INV_ROOT_TWO_PI)


def rows_of(start, count):
    return pl.ds(pl.multiple_of(start, count), count)


def by_rows(count, body):
    def step(i, carry):
        body(rows_of(i * LN_ROWS, LN_ROWS))
        return carry

    lax.fori_loop(0, count // LN_ROWS, step, 0)


def norm_of(total):
    centre = total - jnp.mean(total, axis=-1, keepdims=True)
    factor = lax.rsqrt(jnp.mean(centre * centre, axis=-1, keepdims=True) + EPS)
    return centre * factor, factor


def norm_back(grad, shaped, factor, gain):
    scaled = grad * gain
    centred = scaled - jnp.mean(scaled, axis=-1, keepdims=True)
    return factor * (centred - shaped * jnp.mean(scaled * shaped, axis=-1, keepdims=True))


def both_heads(block):
    first = lax.broadcasted_iota(jnp.int32, block.shape, 1) < HALF
    zero = jnp.zeros_like(block)
    return jnp.concatenate([jnp.where(first, block, zero), jnp.where(first, zero, block)], axis=0)


def attend(unroll, rows, tokens, prefixed, pairs, q, k, vt, vtp, probs, bias, out_t):
    def step(p, carry):
        lanes = rows_of(p * PAIR, PAIR)
        scores = dot_t(k[:, lanes], both_heads(q[:, lanes]))
        shift = bias[...]
        scores = scores + jnp.concatenate([shift] * (2 * rows // PAIR), axis=1)
        power = jnp.exp(scores - jnp.max(scores, axis=0, keepdims=True))
        low = (power * (1.0 / jnp.sum(power, axis=0, keepdims=True))).astype(BF)
        probs(p)[...] = low
        for a in range(2):
            head = rows_of(p * PAIR + a * HALF, HALF)
            part = low[:, a * rows : (a + 1) * rows]
            mixed = dot(vt[head, :], part[:tokens])
            if prefixed:
                mixed = mixed + dot(vtp[head, :], part[tokens:])
            out_t[head, :] = mixed.astype(BF)
        return carry

    lax.fori_loop(0, pairs, step, 0, unroll=unroll)


def attend_back(unroll, rows, tokens, prefixed, pairs, grad, q, k, v, kt, ktp, probs, dq_t, dk, dv, pre_sum):
    def step(p, carry):
        lanes = rows_of(p * PAIR, PAIR)
        grads = both_heads(grad[:, lanes])
        queries = both_heads(q[:, lanes])
        low = probs(p)[...]
        wide = low.astype(F32)
        grad_probs = dot_t(v[:, lanes], grads)
        inner = jnp.sum(wide * grad_probs, axis=0, keepdims=True)
        grad_scores = (wide * (grad_probs - inner)).astype(BF)
        grad_keys = dot(grad_scores, queries)
        grad_values = dot(low, grads)
        dk[:, lanes] = grad_keys[:tokens].astype(BF)
        dv[:, lanes] = grad_values[:tokens].astype(BF)
        if prefixed:
            pre_sum[0, :, lanes] = pre_sum[0, :, lanes] + grad_keys[tokens:]
            pre_sum[1, :, lanes] = pre_sum[1, :, lanes] + grad_values[tokens:]
        for a in range(2):
            head = rows_of(p * PAIR + a * HALF, HALF)
            part = grad_scores[:, a * rows : (a + 1) * rows]
            back = dot(kt[head, :], part[:tokens])
            if prefixed:
                back = back + dot(ktp[head, :], part[tokens:])
            dq_t[head, :] = (back * 0.125).astype(BF)
        return carry

    lax.fori_loop(0, pairs, step, 0, unroll=unroll)


def make_kernel(nz, ny, nx, features, hidden, adapt, src_rows, tgt_rows):
    chunks = hidden // features
    pairs = features // PAIR
    dp = nz * ny * nx
    ra = features // dp
    enc_keys = src_rows + PRE_PAD
    dec_keys = tgt_rows + PRE_PAD
    small_rows = 2 * PRE_PAD

    def kernel(
        src, tgt, ct, sl, tl, ai, ao, cq, cp, co, fi, fo, di, do, bi, bo, prefix, gains,
        tok, ig_out, og_out, sm_out,
        w, wdi, wdo, pw, k, v, kt, tt, ot, ktp, vtp, xh1, xh2, r1, r2, sa, rb, dz, snd, rcv,
        f1, dqkv, rsx, rsy, rsz, rsa, rsb, rsc, pre_sum, bias, ib_sum, ob_sum,
        small, small_in, small_mid, small_z, small_end, small_all,
        dxin, dct, da, kc, vc, kct,
        wsem, xsem, osem, ssem, rsem, gss, grs, mss, mrs,
    ):
        section = lax.axis_index("section")
        here = lax.axis_index("dp")
        at = {"x": lax.rem(here, nx), "y": lax.rem(here // nx, ny), "z": here // (nx * ny)}
        size = {"x": nx, "y": ny, "z": nz}

        def peer(axis, step):
            c = dict(at)
            c[axis] = lax.rem(at[axis] + step, size[axis])
            return c[axis], (section, (c["z"] * ny + c["y"]) * nx + c["x"])

        other = (1 - section, here)
        def remote(source, target, send, receive, device):
            return pltpu.make_async_remote_copy(
                src_ref=source, dst_ref=target, send_sem=send, recv_sem=receive,
                device_id=device, device_id_type=MESH,
            )

        def memory_copy(m, i):
            rows = rows_of(i * PAIR, PAIR)
            return remote(snd.at[rows], rcv.at[m, rows], ssem.at[2 * m + i], rsem.at[2 * m + i], other)

        def back_copy(m, i):
            lanes = pl.ds(i * (features // 2), features // 2)
            return remote(snd.at[:, lanes], rcv.at[m, :, lanes], ssem.at[2 * m + i], rsem.at[2 * m + i], other)

        def greet():
            barrier = pltpu.get_barrier_semaphore()
            partners = [other] + [peer("z", s)[1] for s in range(1, nz)]
            for s in range(1, nx * ny):
                partners.append((section, at["z"] * nx * ny + lax.rem(at["y"] * nx + at["x"] + s, nx * ny)))
            for partner in partners:
                pl.semaphore_signal(barrier, inc=1, device_id=partner, device_id_type=MESH)
            pl.semaphore_wait(barrier, len(partners))

        widths = {"x": nx, "y": ny, "z": nz}
        orders = {"A": "xyz", "B": "yxz"}
        landing = {"A": (rsx, rsy, rsz), "B": (rsa, rsb, rsc)}

        def reduce_phase(part, stage, g):
            axis = orders[part][stage]
            count = ra
            for later in orders[part][stage + 1 :]:
                count *= size[later]
            lanes = slice(0, adapt) if part == "A" else slice(adapt, 2 * adapt)
            copies = []
            base = 0 if part == "A" else 9
            for s in range(1, size[axis]):
                c, device = peer(axis, s)
                rows = rows_of(c * count, count)
                source = g.at[rows, lanes] if stage == 0 else landing[part][stage - 1].at[0, rows]
                i = base + 3 * stage + s - 1
                copies.append(remote(source, landing[part][stage].at[s - 1], gss.at[i], grs.at[i], device))
            return copies

        def reduce_sum(part, stage, g):
            axis = orders[part][stage]
            count = ra
            for later in orders[part][stage + 1 :]:
                count *= size[later]
            lanes = slice(0, adapt) if part == "A" else slice(adapt, 2 * adapt)
            rows = rows_of(at[axis] * count, count)
            mine = g[rows, lanes] if stage == 0 else landing[part][stage - 1][0, rows]
            total = mine.astype(F32)
            for s in range(size[axis] - 1):
                total = total + landing[part][stage][s].astype(F32)
            return total

        def place(d, part):
            z, y, x = lax.div(d, nx * ny), lax.rem(lax.div(d, nx), ny), lax.rem(d, nx)
            if part == "A":
                return pl.multiple_of(((x * ny + y) * nz + z) * ra, ra)
            return pl.multiple_of(((y * nx + x) * nz + z) * ra, ra)

        def write_grads(g, ybs, dfs, count):
            group = 2 * PAIR
            half = ra // 2

            def first(t, carry):
                block = tdot(ybs(rows_of(t * group, group)), dz[0:count])
                for i in range(group // ra):
                    d = t * (group // ra) + i
                    g[pl.ds(place(d, "A"), ra), 0:adapt] = block[i * ra : (i + 1) * ra].astype(BF)
                return carry

            def second(t, carry):
                block = 4.0 * tdot(rb[0:count, rows_of(t * PAIR, PAIR)], dfs())
                for i in range(PAIR // half):
                    d = t * (PAIR // half) + i
                    part = block[i * half : (i + 1) * half]
                    part = jnp.concatenate([part[:, :adapt], part[:, adapt:]], axis=0)
                    g[pl.ds(place(d, "B"), ra), adapt : 2 * adapt] = part.astype(BF)
                return carry

            lax.fori_loop(0, features // group, first, 0)
            lax.fori_loop(0, adapt // PAIR, second, 0)

        def all_start(g, stage):
            for part in "AB":
                for c in reduce_phase(part, stage, g):
                    c.start()

        def all_finish(g, stage):
            for part in "AB":
                for c in reduce_phase(part, stage, g):
                    c.wait()
                total = reduce_sum(part, stage, g)
                if stage < 2:
                    landing[part][stage][0] = total.astype(BF)
                elif part == "A":
                    ig_out[...] = total
                else:
                    half = ra // 2
                    og_out[:, 0:adapt] = total[:half]
                    og_out[:, adapt : 2 * adapt] = total[half:]

        plane = nx * ny
        piece = small_rows * features // (16 * plane)
        across = features // piece
        seat = at["y"] * nx + at["x"]

        def plane_peer(s):
            i = lax.rem(seat + s, plane)
            return i, (section, at["z"] * plane + i)

        def small_at(ref, i):
            return ref.at[rows_of((i // across) * 16, 16), rows_of(lax.rem(i, across) * piece, piece)]

        def small_scatter():
            copies = []
            for s in range(1, plane):
                i, device = plane_peer(s)
                copies.append(remote(small_at(small, i), small_in.at[s - 1], mss.at[s - 1], mrs.at[s - 1], device))
            return copies

        def small_along():
            n = plane - 1
            return [
                remote(small_mid, small_z.at[s - 1], mss.at[n + s - 1], mrs.at[n + s - 1], peer("z", s)[1])
                for s in range(1, nz)
            ]

        def small_gather():
            n = plane - 1 + nz - 1
            copies = []
            for s in range(1, plane):
                device = plane_peer(s)[1]
                copies.append(
                    remote(small_end, small_at(small_all, seat), mss.at[n + s - 1], mrs.at[n + s - 1], device)
                )
            return copies

        def small_begin():
            small[0:PRE_PAD] = pre_sum[0].astype(BF)
            small[PRE_PAD : 2 * PRE_PAD] = pre_sum[1].astype(BF)
            small[PRE : PRE + 1] = ob_sum[...].astype(BF)
            small[PRE_PAD + PRE : PRE_PAD + PRE + 1, 0:adapt] = ib_sum[...].astype(BF)
            for c in small_scatter():
                c.start()

        def small_middle():
            for c in small_scatter():
                c.wait()
            total = small_at(small, seat)[...].astype(F32)
            for s in range(plane - 1):
                total = total + small_in[s].astype(F32)
            small_mid[...] = total.astype(BF)
            for c in small_along():
                c.start()

        def small_late():
            for c in small_along():
                c.wait()
            total = small_mid[...].astype(F32)
            for s in range(nz - 1):
                total = total + small_z[s].astype(F32)
            small_end[...] = total.astype(BF)
            small_at(small_all, seat)[...] = small_end[...]
            for c in small_gather():
                c.start()

        def small_finish():
            for c in small_gather():
                c.wait()
            sm_out[...] = small_all[...].astype(F32)

        blocks = {}
        for b in range(3):
            blocks[b] = (ai.at[0, :, pl.ds(b * features, features)], w.at[b])
        blocks[3] = (ao.at[0], w.at[3])
        for c in range(chunks):
            blocks[4 + c] = (fi.at[0, :, pl.ds(c * features, features)], w.at[4 + c])
            blocks[8 + c] = (fo.at[0, pl.ds(c * features, features), :], w.at[8 + c])
        blocks[12] = (cq, w.at[12])
        blocks[13] = (cp.at[:, pl.ds(0, features)], w.at[13])
        blocks[14] = (cp.at[:, pl.ds(features, features)], w.at[14])
        blocks[15] = (co, w.at[15])
        blocks[16] = (di.at[0], wdi)
        blocks[17] = (do.at[0], wdo)

        def fetch_in(c):
            lanes = rows_of(c * features, features)
            return pltpu.make_async_copy(fi.at[0, :, lanes], w.at[4 + c], wsem.at[4 + c])

        def fetch_out(c):
            rows = rows_of(c * features, features)
            return pltpu.make_async_copy(fo.at[0, rows, :], w.at[8 + c], wsem.at[8 + c])

        def fetch(b):
            return pltpu.make_async_copy(blocks[b][0], blocks[b][1], wsem.at[b])

        def gain(i):
            return gains[0, i : i + 1, :].astype(F32)

        def prefix_setup(tokens):
            pad = jnp.zeros((PRE_PAD, features), BF)
            for m in range(2):
                k[m, pl.ds(tokens, PRE_PAD)] = pad
                v[m, pl.ds(tokens, PRE_PAD)] = pad
                k[m, pl.ds(tokens, PRE)] = prefix[:, 0, :]
                v[m, pl.ds(tokens, PRE)] = prefix[:, 1, :]
            ktp[...] = k[0, pl.ds(tokens, PRE_PAD)].T
            vtp[...] = v[0, pl.ds(tokens, PRE_PAD)].T
            pre_sum[...] = jnp.zeros_like(pre_sum)
            ib_sum[...] = jnp.zeros_like(ib_sum)
            ob_sum[...] = jnp.zeros_like(ob_sum)

        def project(rows, x, q, m):
            q[...] = (dot(x[...], w[0]) * 0.125).astype(BF)
            keys = dot(x[...], w[1]).astype(BF)
            k[m, 0:rows] = keys
            kt[m, :, 0:rows] = keys.T
            values = dot(x[...], w[2]).astype(BF)
            v[m, 0:rows] = values
            tt[:, 0:rows] = values.T

        def branch(unroll, rows, yb, slope, m):
            @pl.when(m == 0)
            def _():
                fetch(16).wait()
                fetch(17).wait()

            pre = dot(yb[...], wdi[...]) + bi[...].astype(F32)
            act, turn = gelu_and_slope(pre)
            act = act.astype(BF)
            rb[rows_of(m * rows, rows)] = act
            sa[m, 0:rows] = turn.astype(BF)
            f1[0:rows] = f1[0:rows] + 4.0 * (dot(act, wdo[...]) + bo[...].astype(F32))

            def step(c, carry):
                @pl.when(m == 0)
                def _():
                    if rows == src_rows:
                        fetch_in(c).wait()
                    fetch_out(c).wait()

                act, turn = gelu_and_slope(dot(yb[...], w[4 + c]))
                slope[1](c, turn.astype(BF))
                f1[0:rows] = f1[0:rows] + dot(act.astype(BF), w[8 + c])
                return carry

            lax.fori_loop(0, chunks, step, 0, unroll=unroll)

        def branch_back_adapter(rows, df, m):
            low = df[...]
            ob_sum[...] = ob_sum[...] + 4.0 * jnp.sum(low.astype(F32), axis=0, keepdims=True)
            grad = ((4.0 * dot_t(low, wdo[...])) * sa[m, 0:rows].astype(F32)).astype(BF)
            dz[rows_of(m * rows, rows)] = grad
            ib_sum[...] = ib_sum[...] + jnp.sum(grad.astype(F32), axis=0, keepdims=True)

        def branch_back_feed(unroll, rows, df, slope, m, turned):
            f1[0:rows] = f1[0:rows] + dot_t(dz[rows_of(m * rows, rows)], wdi[...])

            def step(c, carry):
                grad = (dot_t(df[...], w[8 + c]) * slope[0](c).astype(F32)).astype(BF)
                back = dot(grad, w[c]) if turned else dot_t(grad, w[4 + c])
                f1[0:rows] = f1[0:rows] + back
                return carry

            lax.fori_loop(0, chunks, step, 0, unroll=unroll)

        def self_back(unroll, rows, m, q, between=None):
            def norm(r):
                dt = norm_back(f1[r], xh1[m, r].astype(F32), r1[m, r], gain(0))
                f1[r] = dt
                dqkv[0, r] = dt.astype(BF)

            by_rows(rows, norm)
            ot_rows = dot_t(dqkv[0, 0:rows], w[3]).astype(BF)
            dqkv[0, 0:rows] = ot_rows
            if between is not None:
                between()
            attend_back(
                unroll, rows, rows, True, pairs, dqkv.at[0, pl.ds(0, rows)], q,
                k.at[m, pl.ds(0, rows + PRE_PAD)], v.at[m, pl.ds(0, rows + PRE_PAD)],
                kt.at[m, :, pl.ds(0, rows)], ktp,
                lambda p: pw.at[m, p, pl.ds(0, rows + PRE_PAD), pl.ds(0, 2 * rows)],
                ot.at[:, pl.ds(0, rows)], dqkv.at[1, pl.ds(0, rows)], dqkv.at[2, pl.ds(0, rows)], pre_sum,
            )
            dqkv[0, 0:rows] = ot[:, 0:rows].T

        def self_input(rows, out):
            total = f1[0:rows]
            for b in range(3):
                total = total + dot_t(dqkv[b, 0:rows], w[b])
            out[...] = total.astype(BF)

        def twice(body):
            def step(m, carry):
                body(m)
                return carry

            lax.fori_loop(0, 2, step, 0)

        def xin(m):
            return w.at[15, rows_of(512 + m * src_rows, src_rows)]

        def load_x(m):
            return pltpu.make_async_copy(src.at[m], xin(m), xsem.at[m])

        def load_t(m):
            return pltpu.make_async_copy(tgt.at[m], dxin.at[m], xsem.at[m])

        def load_c(m):
            return pltpu.make_async_copy(ct.at[m], dct.at[m], xsem.at[2 + m])

        def encoder_loads():
            load_x(0).start()
            for b in (0, 1, 2):
                fetch(b).start()
            load_x(1).start()

        def decoder_loads():
            load_t(0).start()
            for b in [0, 1, 2]:
                fetch(b).start()
            load_t(1).start()
            for b in [3, 12, 13, 14, 15, 16, 17, 4, 8, 5, 9, 6, 10, 7, 11]:
                fetch(b).start()
            load_c(0).start()
            load_c(1).start()

        def encoder():
            R = src_rows

            def q(m):
                return w.at[15, rows_of(m * R, R)]

            def yb(m):
                return w.at[14, rows_of(m * R, R)]

            def df(m):
                return w.at[14, rows_of(512 + m * R, R)]

            def slope(m):
                def put(c, value):
                    w[12 + m, rows_of(c * R, R)] = value

                return (lambda c: w[12 + m, rows_of(c * R, R)]), put

            def forward(m):
                load_x(m).wait()

                @pl.when(m == 0)
                def _():
                    fetch(0).wait()
                    for b in (3, 16, 17, 4, 8):
                        fetch(b).start()
                    fetch(1).wait()
                    fetch(2).wait()
                    for b in (5, 9, 6, 10, 7, 11):
                        fetch(b).start()

                project(R, xin(m), q(m), m)
                key = lax.broadcasted_iota(jnp.int32, (enc_keys, PAIR), 0)
                seen = (key < sl[m]) | ((key >= R) & (key < R + PRE))
                bias[...] = jnp.where(seen, 0.0, NEG)
                attend(
                    ENC_PAIRS, R, R, True, pairs, q(m), k.at[m], tt, vtp, lambda p: pw.at[m, p], bias, ot,
                )
                pl.when(m == 0)(fetch(3).wait)
                f1[...] = xin(m)[...].astype(F32) + dot(ot[...].T, w[3])

                def norm(r):
                    shaped, factor = norm_of(f1[r])
                    xh1[m, r] = shaped.astype(BF)
                    r1[m, r] = factor
                    h = shaped * gain(0)
                    f1[r] = h
                    yb(m)[r] = h.astype(BF)

                by_rows(R, norm)
                branch(ENC_CHUNKS, R, yb(m), slope(m), m)


                @pl.when(m == 1)
                def _():
                    for i in range(src_rows // PAIR):
                        memory_copy(0, i).wait_send()

                def last(r):
                    shaped, factor = norm_of(f1[r])
                    xh2[m, r] = shaped.astype(BF)
                    r2[m, r] = factor
                    snd[r] = (shaped * gain(1)).astype(BF)
                    memory_copy(m, r.start // PAIR).start()

                by_rows(R, last)

            def backward(m):

                @pl.when(m == 0)
                def _():
                    for i in range(src_rows // PAIR):
                        memory_copy(1, i).wait_send()

                back_copy(m, 0).wait_recv()
                back_copy(m, 1).wait_recv()

                def norm(r):
                    dt = norm_back(rcv[m, r].astype(F32), xh2[m, r].astype(F32), r2[m, r], gain(1))
                    f1[r] = dt
                    df(m)[r] = dt.astype(BF)

                by_rows(R, norm)
                branch_back_adapter(R, df(m), m)
                g = w.at[12]

                @pl.when(m == 1)
                def _():
                    write_grads(g, lambda r: w[14, 0 : 2 * R, r], lambda: w[14, 512 : 512 + 2 * R], 2 * R)
                    all_start(g, 0)

                branch_back_feed(ENC_CHUNKS, R, df(m), slope(m), m, False)

                def between():
                    @pl.when(m == 1)
                    def _():
                        all_finish(g, 0)
                        all_start(g, 1)

                self_back(ENC_PAIRS, R, m, q(m), between)

                @pl.when(m == 1)
                def _():
                    small_begin()

                self_input(R, xin(m))

                @pl.when(m == 1)
                def _():
                    all_finish(g, 1)
                    small_middle()
                    all_start(g, 2)

                store_x(m).start()

            def store_x(m):
                return pltpu.make_async_copy(xin(m), tok.at[0, m], osem.at[m])

            prefix_setup(R)
            twice(forward)
            twice(backward)
            small_late()
            all_finish(w.at[12], 2)
            store_x(0).wait()
            store_x(1).wait()
            small_finish()

        def decoder():
            R = tgt_rows

            def shifted(r):
                return pl.ds(pl.multiple_of(r.start + R, LN_ROWS), LN_ROWS)

            def pick(c):
                parts = [pw[1, 2 * c + i // 2, pl.ds((i % 2) * R, R), 256:512] for i in range(4)]
                return jnp.concatenate(parts, axis=1)

            def put(c, value):
                for i in range(4):
                    pw[1, 2 * c + i // 2, pl.ds((i % 2) * R, R), 256:512] = value[:, 256 * i : 256 * (i + 1)]

            slope = (pick, put)

            def early(m):
                return da.at[m]

            def dq_(m):
                return k.at[m, pl.ds(dec_keys, R)]

            def dqc_(m):
                return v.at[m, pl.ds(dec_keys, R)]

            def self_probs(m):
                return lambda p: pw.at[m, p, pl.ds(0, dec_keys), pl.ds(0, 2 * R)]

            def cross_probs():
                return lambda p: pw.at[0, p, pl.ds(0, src_rows), pl.ds(2 * R, 2 * R)]

            def self_forward(m):
                load_t(m).wait()

                @pl.when(m == 0)
                def _():
                    for b in range(3):
                        fetch(b).wait()

                project(R, dxin.at[m], dq_(m), m)
                key = lax.broadcasted_iota(jnp.int32, (dec_keys, PAIR), 0)
                query = lax.broadcasted_iota(jnp.int32, (dec_keys, PAIR), 1)
                seen = (key <= query) | ((key >= R) & (key < R + PRE))
                bias[0:dec_keys] = jnp.where(seen, 0.0, NEG)
                attend(
                    SELF_PAIRS, R, R, True, pairs, dq_(m), k.at[m, pl.ds(0, dec_keys)],
                    tt.at[:, pl.ds(0, R)], vtp, self_probs(m), bias.at[pl.ds(0, dec_keys)],
                    ot.at[:, pl.ds(0, R)],
                )
                pl.when(m == 0)(fetch(3).wait)
                f1[0:R] = dxin[m].astype(F32) + dot(ot[:, 0:R].T, w[3])

                def norm(r):
                    shaped, factor = norm_of(f1[r])
                    xh1[m, r] = shaped.astype(BF)
                    r1[m, r] = factor
                    h = shaped * gain(0)
                    early(m)[r] = h
                    xh1[m, shifted(r)] = h.astype(BF)

                by_rows(R, norm)
                pl.when(m == 0)(fetch(12).wait)
                dqc_(m)[...] = (dot(xh1[m, R : 2 * R], w[12]) * 0.125).astype(BF)

            def middle(m):
                for i in range(src_rows // PAIR):
                    memory_copy(m, i).wait_recv()

                @pl.when(m == 0)
                def _():
                    fetch(13).wait()
                    fetch(14).wait()

                keys = dot(rcv[m], w[13]).astype(BF)
                kc[...] = keys
                kct[...] = keys.T
                values = dot(rcv[m], w[14]).astype(BF)
                vc[...] = values
                tt[...] = values.T
                key = lax.broadcasted_iota(jnp.int32, (src_rows, PAIR), 0)
                bias[0:src_rows] = jnp.where(key < sl[m], 0.0, NEG)
                attend(
                    CROSS_PAIRS, R, src_rows, False, pairs, dqc_(m), kc, tt, None, cross_probs(),
                    bias.at[pl.ds(0, src_rows)], ot.at[:, pl.ds(0, R)],
                )
                pl.when(m == 0)(fetch(15).wait)
                f1[0:R] = early(m)[...] + dot(ot[:, 0:R].T, w[15])
                yb = xh1.at[m, pl.ds(R, R)]

                def norm(r):
                    shaped, factor = norm_of(f1[r])
                    xh2[m, r] = shaped.astype(BF)
                    r2[m, r] = factor
                    h = shaped * gain(1)
                    f1[r] = h
                    yb[r] = h.astype(BF)

                by_rows(R, norm)
                branch(DEC_CHUNKS, R, yb, slope, m)
                load_c(m).wait()
                df = xh2.at[m, pl.ds(R, R)]

                def turn(r):
                    shaped, factor = norm_of(f1[r])
                    row = lax.broadcasted_iota(jnp.int32, (LN_ROWS, 1), 0) + r.start
                    on = jnp.where(row < tl[m], 1.0, 0.0)
                    grad = dct[m, r].astype(F32) * on
                    dct[m, r] = (shaped * gain(2) * on).astype(BF)
                    dt = norm_back(grad, shaped, factor, gain(2))
                    f1[r] = dt
                    df[r] = dt.astype(BF)

                by_rows(R, turn)
                store_d(m).start()
                branch_back_adapter(R, df, m)
                branch_back_feed(DEC_CHUNKS, R, df, slope, m, True)

                @pl.when(m == 1)
                def _():
                    for b in range(4):
                        fetch(b).start()
                    write_grads(
                        g,
                        lambda r: xh1[:, R : 2 * R, r].reshape(2 * R, 2 * PAIR),
                        lambda: xh2[:, R : 2 * R].reshape(2 * R, features),
                        2 * R,
                    )
                    all_start(g, 0)

                def back(r):
                    dt = norm_back(f1[r], xh2[m, r].astype(F32), r2[m, r], gain(1))
                    f1[r] = dt
                    dqkv[0, r] = dt.astype(BF)

                by_rows(R, back)
                grad_mixed = dot_t(dqkv[0, 0:R], w[15]).astype(BF)
                dqkv[0, 0:R] = grad_mixed
                attend_back(
                    CROSS_PAIRS, R, src_rows, False, pairs, dqkv.at[0, pl.ds(0, R)], dqc_(m), kc, vc, kct, None,
                    cross_probs(), kt.at[m, :, pl.ds(R, R)], dqkv.at[1], dqkv.at[2], None,
                )

                @pl.when(m == 1)
                def _():
                    back_copy(0, 0).wait_send()
                    back_copy(0, 1).wait_send()

                span = features // 2
                for i in range(2):
                    part = pl.ds(i * span, span)
                    snd[:, part] = (dot_t(dqkv[1], w[13, part]) + dot_t(dqkv[2], w[14, part])).astype(BF)
                    back_copy(m, i).start()
                early(m)[...] = f1[0:R]

            def store_d(m):
                return pltpu.make_async_copy(dct.at[m], tok.at[0, m, pl.ds(0, R)], osem.at[m])

            def store_y(m):
                return pltpu.make_async_copy(dxin.at[m], tok.at[0, m, pl.ds(R, R)], osem.at[2 + m])

            g = w.at[8]
            prefix_setup(R)
            twice(self_forward)

            def turn_block(c, carry):
                fetch_in(c).wait()
                w[c] = w[4 + c].T
                return carry

            lax.fori_loop(0, chunks, turn_block, 0)
            twice(middle)
            all_finish(g, 0)
            all_start(g, 1)
            for b in range(4):
                fetch(b).wait()

            def last(m):
                f1[0:R] = early(m)[...] + dot_t(kt[m, :, R : 2 * R].T, w[12])
                self_back(SELF_PAIRS, R, m, dq_(m))
                pl.when(m == 1)(small_begin)
                self_input(R, dxin.at[m])
                store_y(m).start()

                @pl.when(m == 0)
                def _():
                    all_finish(g, 1)
                    all_start(g, 2)

            twice(last)
            small_middle()
            all_finish(g, 2)
            small_late()
            for m in range(2):
                store_d(m).wait()
                store_y(m).wait()
            back_copy(1, 0).wait_send()
            back_copy(1, 1).wait_send()
            small_finish()

        @pl.when(section == 0)
        def _():
            encoder_loads()

        @pl.when(section == 1)
        def _():
            decoder_loads()

        greet()
        pl.when(section == 0)(encoder)
        pl.when(section == 1)(decoder)

    vm = pltpu.VMEM
    plane = nx * ny
    piece = small_rows * features // (16 * plane)
    smalls = 2 * (plane - 1) + nz - 1
    scratch = [
        vm((16, features, features), BF),
        vm((features, adapt), BF),
        vm((adapt, features), BF),
        vm((2, pairs, enc_keys, 2 * src_rows), BF),
        vm((2, enc_keys, features), BF),
        vm((2, enc_keys, features), BF),
        vm((2, features, src_rows), BF),
        vm((features, src_rows), BF),
        vm((features, src_rows), BF),
        vm((features, PRE_PAD), BF),
        vm((features, PRE_PAD), BF),
        vm((2, src_rows, features), BF),
        vm((2, src_rows, features), BF),
        vm((2, src_rows, 1), F32),
        vm((2, src_rows, 1), F32),
        vm((2, src_rows, adapt), BF),
        vm((2 * src_rows, adapt), BF),
        vm((2 * src_rows, adapt), BF),
        vm((src_rows, features), BF),
        vm((2, src_rows, features), BF),
        vm((src_rows, features), F32),
        vm((3, src_rows, features), BF),
        vm((nx - 1, ny * nz * ra, adapt), BF),
        vm((ny - 1, nz * ra, adapt), BF),
        vm((nz - 1, ra, adapt), BF),
        vm((ny - 1, nx * nz * ra, adapt), BF),
        vm((nx - 1, nz * ra, adapt), BF),
        vm((nz - 1, ra, adapt), BF),
        vm((2, PRE_PAD, features), F32),
        vm((enc_keys, PAIR), F32),
        vm((1, adapt), F32),
        vm((1, features), F32),
        vm((small_rows, features), BF),
        vm((plane - 1, 16, piece), BF),
        vm((16, piece), BF),
        vm((nz - 1, 16, piece), BF),
        vm((16, piece), BF),
        vm((small_rows, features), BF),
        vm((2, tgt_rows, features), BF),
        vm((2, tgt_rows, features), BF),
        vm((2, tgt_rows, features), F32),
        vm((src_rows, features), BF),
        vm((src_rows, features), BF),
        vm((features, src_rows), BF),
        pltpu.SemaphoreType.DMA((18,)),
        pltpu.SemaphoreType.DMA((4,)),
        pltpu.SemaphoreType.DMA((4,)),
        pltpu.SemaphoreType.DMA((4,)),
        pltpu.SemaphoreType.DMA((4,)),
        pltpu.SemaphoreType.DMA((18,)),
        pltpu.SemaphoreType.DMA((18,)),
        pltpu.SemaphoreType.DMA((smalls,)),
        pltpu.SemaphoreType.DMA((smalls,)),
    ]
    return kernel, scratch, ra


def finish(tok, ig, og, small, tok_out, pre_out, ig_out, og_out, ib_out, ob_out, sem):
    copy = pltpu.make_async_copy(tok, tok_out, sem)
    copy.start()
    adapt = ig.shape[1]
    pre_out[:, 0, :] = small[0:PRE]
    pre_out[:, 1, :] = small[PRE_PAD : PRE_PAD + PRE]
    ig_out[0] = ig[...]
    og_out[0] = og[...]
    ob_out[...] = small[PRE : PRE + 1]
    ib_out[...] = small[PRE_PAD + PRE : PRE_PAD + PRE + 1, 0:adapt]
    copy.wait()


def solution(mesh):
    dp = mesh.shape["dp"]
    nz = 4
    nx = math.isqrt(dp // nz)
    ny = dp // (nz * nx)

    def per_device(
        source, target, cotangent, source_lengths, target_lengths, attention_in, attention_out,
        cross_query, cross_pair, cross_output, feed_in, feed_out, adapter_in, adapter_in_bias,
        adapter_out, adapter_out_bias, prefix, norm_gains,
    ):
        features = source.shape[2]
        adapt = adapter_in.shape[2]
        kernel, scratch, ra = make_kernel(
            nz, ny, nx, features, feed_in.shape[2], adapt, source.shape[1], target.shape[1]
        )
        anywhere = pl.BlockSpec(memory_space=pl.ANY)
        scalar = pl.BlockSpec(memory_space=pltpu.SMEM)
        vector = pl.BlockSpec(memory_space=pltpu.VMEM)
        tok, ig, og, small = pl.pallas_call(
            kernel,
            out_shape=(
                jax.ShapeDtypeStruct((1, source.shape[0], source.shape[1], features), BF),
                jax.ShapeDtypeStruct((ra, adapt), F32),
                jax.ShapeDtypeStruct((ra // 2, features), F32),
                jax.ShapeDtypeStruct((2 * PRE_PAD, features), F32),
            ),
            in_specs=[anywhere] * 3 + [scalar] * 2 + [anywhere] * 9 + [vector] * 4,
            out_specs=(anywhere, vector, vector, vector),
            scratch_shapes=scratch,
            compiler_params=pltpu.CompilerParams(
                collective_id=0, has_side_effects=True, vmem_limit_bytes=67000000
            ),
        )(
            source, target, cotangent, source_lengths.reshape(-1), target_lengths.reshape(-1), attention_in,
            attention_out, cross_query, cross_pair, cross_output, feed_in, feed_out, adapter_in, adapter_out,
            adapter_in_bias, adapter_out_bias, prefix[0].transpose(1, 0, 2), norm_gains,
        )
        tok, pre, ig, og, ib, ob = pl.pallas_call(
            finish,
            out_shape=(
                jax.ShapeDtypeStruct(tok.shape, BF),
                jax.ShapeDtypeStruct((PRE, 2, features), F32),
                jax.ShapeDtypeStruct((1, ra, adapt), F32),
                jax.ShapeDtypeStruct((1, ra // 2, features), F32),
                jax.ShapeDtypeStruct((1, adapt), F32),
                jax.ShapeDtypeStruct((1, features), F32),
            ),
            in_specs=[anywhere, vector, vector, vector],
            out_specs=(vector, vector, vector, vector, vector, vector),
            scratch_shapes=[pltpu.SemaphoreType.DMA(())],
        )(tok, ig, og, small)
        return tok, pre.transpose(1, 0, 2)[None], ig, og, ib, ob

    return jax.shard_map(
        per_device,
        mesh=mesh,
        in_specs=(
            P(None, "dp", None),
            P(None, "dp", None),
            P(None, "dp", None),
            P(None, "dp"),
            P(None, "dp"),
            P("section", None, None),
            P("section", None, None),
            P(),
            P(),
            P(),
            P("section", None, None),
            P("section", None, None),
            P("section", None, None),
            P("section", None),
            P("section", None, None),
            P("section", None),
            P("section", None, None, None),
            P("section", None, None),
        ),
        out_specs=(
            P("section", None, "dp", None),
            P("section", None, None, None),
            P("section", "dp", None),
            P("section", "dp", None),
            P("section", None),
            P("section", None),
        ),
        check_vma=False,
    )
```

```python
import math

import jax
import jax.numpy as jnp
from jax import lax
from jax.experimental import pallas as pl
from jax.experimental.pallas import tpu as pltpu
from jax.sharding import PartitionSpec as P

BF = jnp.bfloat16
F32 = jnp.float32
MESH = pl.DeviceIdType.MESH
EPS = 1e-05
NEG = -1e30
ROOT_HALF = 0.7071067811865476
INV_ROOT_TWO_PI = 0.3989422804014327
PRE = 30
PRE_PAD = 32
PAIR = 128
HALF = 64
LN_ROWS = 128
ENC_PAIRS = 8
SELF_PAIRS = 2
CROSS_PAIRS = 8
ENC_CHUNKS = 1
DEC_CHUNKS = 4
ENC_GRADS = 1
DEC_GRADS = 4


def dot(a, b):
    return jnp.dot(a, b, preferred_element_type=F32)


def dot_t(a, b):
    return lax.dot_general(a, b, (((1,), (1,)), ((), ())), preferred_element_type=F32)


def tdot(a, b):
    return lax.dot_general(a, b, (((0,), (0,)), ((), ())), preferred_element_type=F32)


def gelu_and_slope(v):
    cdf = 0.5 + 0.5 * lax.erf(v * ROOT_HALF)
    return v * cdf, cdf + v * (jnp.exp(-0.5 * v * v) * INV_ROOT_TWO_PI)


def rows_of(start, count):
    return pl.ds(pl.multiple_of(start, count), count)


def by_rows(count, body):
    def step(i, carry):
        body(rows_of(i * LN_ROWS, LN_ROWS))
        return carry

    lax.fori_loop(0, count // LN_ROWS, step, 0)


def norm_of(total):
    centre = total - jnp.mean(total, axis=-1, keepdims=True)
    factor = lax.rsqrt(jnp.mean(centre * centre, axis=-1, keepdims=True) + EPS)
    return centre * factor, factor


def norm_back(grad, shaped, factor, gain):
    scaled = grad * gain
    centred = scaled - jnp.mean(scaled, axis=-1, keepdims=True)
    return factor * (centred - shaped * jnp.mean(scaled * shaped, axis=-1, keepdims=True))


def both_heads(block):
    first = lax.broadcasted_iota(jnp.int32, block.shape, 1) < HALF
    zero = jnp.zeros_like(block)
    return jnp.concatenate([jnp.where(first, block, zero), jnp.where(first, zero, block)], axis=0)


def attend(unroll, rows, tokens, prefixed, pairs, q, k, vt, vtp, probs, bias, out_t):
    def step(p, carry):
        lanes = rows_of(p * PAIR, PAIR)
        scores = dot_t(k[:, lanes], both_heads(q[:, lanes]))
        shift = bias[...]
        scores = scores + jnp.concatenate([shift] * (2 * rows // PAIR), axis=1)
        power = jnp.exp(scores - jnp.max(scores, axis=0, keepdims=True))
        low = (power * (1.0 / jnp.sum(power, axis=0, keepdims=True))).astype(BF)
        probs(p)[...] = low
        for a in range(2):
            head = rows_of(p * PAIR + a * HALF, HALF)
            part = low[:, a * rows : (a + 1) * rows]
            mixed = dot(vt[head, :], part[:tokens])
            if prefixed:
                mixed = mixed + dot(vtp[head, :], part[tokens:])
            out_t[head, :] = mixed.astype(BF)
        return carry

    lax.fori_loop(0, pairs, step, 0, unroll=unroll)


def attend_back(unroll, rows, tokens, prefixed, pairs, grad, q, k, v, kt, ktp, probs, dq_t, dk, dv, pre_sum):
    def step(p, carry):
        lanes = rows_of(p * PAIR, PAIR)
        grads = both_heads(grad[:, lanes])
        queries = both_heads(q[:, lanes])
        low = probs(p)[...]
        wide = low.astype(F32)
        grad_probs = dot_t(v[:, lanes], grads)
        inner = jnp.sum(wide * grad_probs, axis=0, keepdims=True)
        grad_scores = (wide * (grad_probs - inner)).astype(BF)
        grad_keys = dot(grad_scores, queries)
        grad_values = dot(low, grads)
        dk[:, lanes] = grad_keys[:tokens].astype(BF)
        dv[:, lanes] = grad_values[:tokens].astype(BF)
        if prefixed:
            pre_sum[0, :, lanes] = pre_sum[0, :, lanes] + grad_keys[tokens:]
            pre_sum[1, :, lanes] = pre_sum[1, :, lanes] + grad_values[tokens:]
        for a in range(2):
            head = rows_of(p * PAIR + a * HALF, HALF)
            part = grad_scores[:, a * rows : (a + 1) * rows]
            back = dot(kt[head, :], part[:tokens])
            if prefixed:
                back = back + dot(ktp[head, :], part[tokens:])
            dq_t[head, :] = (back * 0.125).astype(BF)
        return carry

    lax.fori_loop(0, pairs, step, 0, unroll=unroll)


def make_kernel(nz, ny, nx, features, hidden, adapt, src_rows, tgt_rows):
    chunks = hidden // features
    pairs = features // PAIR
    dp = nz * ny * nx
    ra = features // dp
    enc_keys = src_rows + PRE_PAD
    dec_keys = tgt_rows + PRE_PAD
    small_rows = 2 * PRE_PAD

    def kernel(
        src, tgt, ct, sl, tl, ai, ao, cq, cp, co, fi, fo, di, do, bi, bo, prefix, gains,
        tok, ig_out, og_out, sm_out,
        w, wdi, wdo, pw, k, v, kt, tt, ot, ktp, vtp, xh1, xh2, r1, r2, sa, rb, dz, snd, rcv,
        f1, dqkv, rsx, rsy, rsz, rsa, rsb, rsc, pre_sum, bias, ib_sum, ob_sum,
        small, small_in, small_mid, small_z, small_end, small_all,
        dxin, dct, da, kc, vc, kct,
        wsem, xsem, osem, ssem, rsem, gss, grs, mss, mrs,
    ):
        section = lax.axis_index("section")
        here = lax.axis_index("dp")
        at = {"x": lax.rem(here, nx), "y": lax.rem(here // nx, ny), "z": here // (nx * ny)}
        size = {"x": nx, "y": ny, "z": nz}

        def peer(axis, step):
            c = dict(at)
            c[axis] = lax.rem(at[axis] + step, size[axis])
            return c[axis], (section, (c["z"] * ny + c["y"]) * nx + c["x"])

        other = (1 - section, here)
        def remote(source, target, send, receive, device):
            return pltpu.make_async_remote_copy(
                src_ref=source, dst_ref=target, send_sem=send, recv_sem=receive,
                device_id=device, device_id_type=MESH,
            )

        def memory_copy(m, i):
            rows = rows_of(i * PAIR, PAIR)
            return remote(snd.at[rows], rcv.at[m, rows], ssem.at[2 * m + i], rsem.at[2 * m + i], other)

        def back_copy(m, i):
            lanes = pl.ds(i * (features // 2), features // 2)
            return remote(snd.at[:, lanes], rcv.at[m, :, lanes], ssem.at[2 * m + i], rsem.at[2 * m + i], other)

        def greet():
            barrier = pltpu.get_barrier_semaphore()
            partners = [other] + [peer("z", s)[1] for s in range(1, nz)]
            for s in range(1, nx * ny):
                partners.append((section, at["z"] * nx * ny + lax.rem(at["y"] * nx + at["x"] + s, nx * ny)))
            for partner in partners:
                pl.semaphore_signal(barrier, inc=1, device_id=partner, device_id_type=MESH)
            pl.semaphore_wait(barrier, len(partners))

        widths = {"x": nx, "y": ny, "z": nz}
        orders = {"A": "xyz", "B": "yxz"}
        landing = {"A": (rsx, rsy, rsz), "B": (rsa, rsb, rsc)}

        def reduce_phase(part, stage, g):
            axis = orders[part][stage]
            count = ra
            for later in orders[part][stage + 1 :]:
                count *= size[later]
            lanes = slice(0, adapt) if part == "A" else slice(adapt, 2 * adapt)
            copies = []
            base = 0 if part == "A" else 9
            for s in range(1, size[axis]):
                c, device = peer(axis, s)
                rows = rows_of(c * count, count)
                source = g.at[rows, lanes] if stage == 0 else landing[part][stage - 1].at[0, rows]
                i = base + 3 * stage + s - 1
                copies.append(remote(source, landing[part][stage].at[s - 1], gss.at[i], grs.at[i], device))
            return copies

        def reduce_sum(part, stage, g):
            axis = orders[part][stage]
            count = ra
            for later in orders[part][stage + 1 :]:
                count *= size[later]
            lanes = slice(0, adapt) if part == "A" else slice(adapt, 2 * adapt)
            rows = rows_of(at[axis] * count, count)
            mine = g[rows, lanes] if stage == 0 else landing[part][stage - 1][0, rows]
            total = mine.astype(F32)
            for s in range(size[axis] - 1):
                total = total + landing[part][stage][s].astype(F32)
            return total

        def place(d, part):
            z, y, x = lax.div(d, nx * ny), lax.rem(lax.div(d, nx), ny), lax.rem(d, nx)
            if part == "A":
                return pl.multiple_of(((x * ny + y) * nz + z) * ra, ra)
            return pl.multiple_of(((y * nx + x) * nz + z) * ra, ra)

        def write_in(unroll, g, ybs, count):
            group = 2 * PAIR

            def step(t, carry):
                block = tdot(ybs(rows_of(t * group, group)), dz[0:count])
                for i in range(group // ra):
                    d = t * (group // ra) + i
                    g[pl.ds(place(d, "A"), ra), 0:adapt] = block[i * ra : (i + 1) * ra].astype(BF)
                return carry

            lax.fori_loop(0, features // group, step, 0, unroll=unroll)

        def write_out(unroll, g, dfs, count):
            half = ra // 2

            def step(t, carry):
                block = 4.0 * tdot(rb[0:count, rows_of(t * PAIR, PAIR)], dfs())
                for i in range(PAIR // half):
                    d = t * (PAIR // half) + i
                    part = block[i * half : (i + 1) * half]
                    part = jnp.concatenate([part[:, :adapt], part[:, adapt:]], axis=0)
                    g[pl.ds(place(d, "B"), ra), adapt : 2 * adapt] = part.astype(BF)
                return carry

            lax.fori_loop(0, adapt // PAIR, step, 0, unroll=unroll)

        def start(part, stage, g):
            for c in reduce_phase(part, stage, g):
                c.start()

        def finish_stage(part, stage, g):
            for c in reduce_phase(part, stage, g):
                c.wait()
            total = reduce_sum(part, stage, g)
            if stage < 2:
                landing[part][stage][0] = total.astype(BF)
                start(part, stage + 1, g)
            elif part == "A":
                ig_out[...] = total
            else:
                half = ra // 2
                og_out[:, 0:adapt] = total[:half]
                og_out[:, adapt : 2 * adapt] = total[half:]

        def finish_both(stage, g):
            finish_stage("B", stage, g)
            finish_stage("A", stage, g)

        plane = nx * ny
        piece = small_rows * features // (16 * plane)
        across = features // piece
        seat = at["y"] * nx + at["x"]

        def plane_peer(s):
            i = lax.rem(seat + s, plane)
            return i, (section, at["z"] * plane + i)

        def small_at(ref, i):
            return ref.at[rows_of((i // across) * 16, 16), rows_of(lax.rem(i, across) * piece, piece)]

        def small_scatter():
            copies = []
            for s in range(1, plane):
                i, device = plane_peer(s)
                copies.append(remote(small_at(small, i), small_in.at[s - 1], mss.at[s - 1], mrs.at[s - 1], device))
            return copies

        def small_along():
            n = plane - 1
            return [
                remote(small_mid, small_z.at[s - 1], mss.at[n + s - 1], mrs.at[n + s - 1], peer("z", s)[1])
                for s in range(1, nz)
            ]

        def small_gather():
            n = plane - 1 + nz - 1
            copies = []
            for s in range(1, plane):
                device = plane_peer(s)[1]
                copies.append(
                    remote(small_end, small_at(small_all, seat), mss.at[n + s - 1], mrs.at[n + s - 1], device)
                )
            return copies

        def small_begin():
            small[0:PRE_PAD] = pre_sum[0].astype(BF)
            small[PRE_PAD : 2 * PRE_PAD] = pre_sum[1].astype(BF)
            small[PRE : PRE + 1] = ob_sum[...].astype(BF)
            small[PRE_PAD + PRE : PRE_PAD + PRE + 1, 0:adapt] = ib_sum[...].astype(BF)
            for c in small_scatter():
                c.start()

        def small_middle():
            for c in small_scatter():
                c.wait()
            total = small_at(small, seat)[...].astype(F32)
            for s in range(plane - 1):
                total = total + small_in[s].astype(F32)
            small_mid[...] = total.astype(BF)
            for c in small_along():
                c.start()

        def small_late():
            for c in small_along():
                c.wait()
            total = small_mid[...].astype(F32)
            for s in range(nz - 1):
                total = total + small_z[s].astype(F32)
            small_end[...] = total.astype(BF)
            small_at(small_all, seat)[...] = small_end[...]
            for c in small_gather():
                c.start()

        def small_finish():
            for c in small_gather():
                c.wait()
            sm_out[...] = small_all[...].astype(F32)

        blocks = {}
        for b in range(3):
            blocks[b] = (ai.at[0, :, pl.ds(b * features, features)], w.at[b])
        blocks[3] = (ao.at[0], w.at[3])
        for c in range(chunks):
            blocks[4 + c] = (fi.at[0, :, pl.ds(c * features, features)], w.at[4 + c])
            blocks[8 + c] = (fo.at[0, pl.ds(c * features, features), :], w.at[8 + c])
        blocks[12] = (cq, w.at[12])
        blocks[13] = (cp.at[:, pl.ds(0, features)], w.at[13])
        blocks[14] = (cp.at[:, pl.ds(features, features)], w.at[14])
        blocks[15] = (co, w.at[15])
        blocks[16] = (di.at[0], wdi)
        blocks[17] = (do.at[0], wdo)

        def fetch_in(c):
            lanes = rows_of(c * features, features)
            return pltpu.make_async_copy(fi.at[0, :, lanes], w.at[4 + c], wsem.at[4 + c])

        def fetch_out(c):
            rows = rows_of(c * features, features)
            return pltpu.make_async_copy(fo.at[0, rows, :], w.at[8 + c], wsem.at[8 + c])

        def fetch(b):
            return pltpu.make_async_copy(blocks[b][0], blocks[b][1], wsem.at[b])

        def gain(i):
            return gains[0, i : i + 1, :].astype(F32)

        def prefix_setup(tokens):
            pad = jnp.zeros((PRE_PAD, features), BF)
            for m in range(2):
                k[m, pl.ds(tokens, PRE_PAD)] = pad
                v[m, pl.ds(tokens, PRE_PAD)] = pad
                k[m, pl.ds(tokens, PRE)] = prefix[:, 0, :]
                v[m, pl.ds(tokens, PRE)] = prefix[:, 1, :]
            ktp[...] = k[0, pl.ds(tokens, PRE_PAD)].T
            vtp[...] = v[0, pl.ds(tokens, PRE_PAD)].T
            pre_sum[...] = jnp.zeros_like(pre_sum)
            ib_sum[...] = jnp.zeros_like(ib_sum)
            ob_sum[...] = jnp.zeros_like(ob_sum)

        def project(rows, x, q, m):
            q[...] = (dot(x[...], w[0]) * 0.125).astype(BF)
            keys = dot(x[...], w[1]).astype(BF)
            k[m, 0:rows] = keys
            kt[m, :, 0:rows] = keys.T
            values = dot(x[...], w[2]).astype(BF)
            v[m, 0:rows] = values
            tt[:, 0:rows] = values.T

        def branch(unroll, rows, yb, slope, m):
            pre = dot(yb[...], wdi[...]) + bi[...].astype(F32)
            act, turn = gelu_and_slope(pre)
            act = act.astype(BF)
            rb[rows_of(m * rows, rows)] = act
            sa[m, 0:rows] = turn.astype(BF)
            f1[0:rows] = f1[0:rows] + 4.0 * (dot(act, wdo[...]) + bo[...].astype(F32))

            if rows == src_rows:

                @pl.when(m == 0)
                def _():
                    for b in (4, 8, 5, 9, 6, 10, 7, 11):
                        fetch(b).wait()

            def step(c, carry):
                act, turn = gelu_and_slope(dot(yb[...], w[4 + c]))
                slope[1](c, turn.astype(BF))
                f1[0:rows] = f1[0:rows] + dot(act.astype(BF), w[8 + c])
                return carry

            lax.fori_loop(0, chunks, step, 0, unroll=unroll)

        def branch_back_adapter(rows, df, m):
            low = df[...]
            ob_sum[...] = ob_sum[...] + 4.0 * jnp.sum(low.astype(F32), axis=0, keepdims=True)
            grad = ((4.0 * dot_t(low, wdo[...])) * sa[m, 0:rows].astype(F32)).astype(BF)
            dz[rows_of(m * rows, rows)] = grad
            ib_sum[...] = ib_sum[...] + jnp.sum(grad.astype(F32), axis=0, keepdims=True)

        def branch_back_feed(unroll, rows, df, slope, m, turned):
            f1[0:rows] = f1[0:rows] + dot_t(dz[rows_of(m * rows, rows)], wdi[...])

            def step(c, carry):
                grad = (dot_t(df[...], w[8 + c]) * slope[0](c).astype(F32)).astype(BF)
                back = dot(grad, w[c]) if turned else dot_t(grad, w[4 + c])
                f1[0:rows] = f1[0:rows] + back
                return carry

            lax.fori_loop(0, chunks, step, 0, unroll=unroll)

        def self_back(unroll, rows, m, q, between=None):
            def norm(r):
                dt = norm_back(f1[r], xh1[m, r].astype(F32), r1[m, r], gain(0))
                f1[r] = dt
                dqkv[0, r] = dt.astype(BF)

            by_rows(rows, norm)
            ot_rows = dot_t(dqkv[0, 0:rows], w[3]).astype(BF)
            dqkv[0, 0:rows] = ot_rows
            if between is not None:
                between()
            attend_back(
                unroll, rows, rows, True, pairs, dqkv.at[0, pl.ds(0, rows)], q,
                k.at[m, pl.ds(0, rows + PRE_PAD)], v.at[m, pl.ds(0, rows + PRE_PAD)],
                kt.at[m, :, pl.ds(0, rows)], ktp,
                lambda p: pw.at[m, p, pl.ds(0, rows + PRE_PAD), pl.ds(0, 2 * rows)],
                ot.at[:, pl.ds(0, rows)], dqkv.at[1, pl.ds(0, rows)], dqkv.at[2, pl.ds(0, rows)], pre_sum,
            )
            dqkv[0, 0:rows] = ot[:, 0:rows].T

        def self_input(rows, out):
            total = f1[0:rows]
            for b in range(3):
                total = total + dot_t(dqkv[b, 0:rows], w[b])
            out[...] = total.astype(BF)

        def twice(body):
            def step(m, carry):
                body(m)
                return carry

            lax.fori_loop(0, 2, step, 0)

        def xin(m):
            return w.at[15, rows_of(512 + m * src_rows, src_rows)]

        def load_x(m):
            return pltpu.make_async_copy(src.at[m], xin(m), xsem.at[m])

        def load_t(m):
            return pltpu.make_async_copy(tgt.at[m], dxin.at[m], xsem.at[m])

        def load_c(m):
            return pltpu.make_async_copy(ct.at[m], dct.at[m], xsem.at[2 + m])

        def encoder_loads():
            load_x(0).start()
            for b in (0, 1, 2):
                fetch(b).start()
            load_x(1).start()

        def decoder_loads():
            load_t(0).start()
            for b in [0, 1, 2]:
                fetch(b).start()
            load_t(1).start()

        def encoder():
            R = src_rows

            def q(m):
                return w.at[15, rows_of(m * R, R)]

            def yb(m):
                return w.at[14, rows_of(m * R, R)]

            def df(m):
                return w.at[14, rows_of(512 + m * R, R)]

            def slope(m):
                def put(c, value):
                    w[12 + m, rows_of(c * R, R)] = value

                return (lambda c: w[12 + m, rows_of(c * R, R)]), put

            def forward(m):
                load_x(m).wait()

                @pl.when(m == 0)
                def _():
                    fetch(0).wait()
                    for b in (3, 16, 17, 4, 8):
                        fetch(b).start()
                    fetch(1).wait()
                    fetch(2).wait()
                    for b in (5, 9, 6, 10, 7, 11):
                        fetch(b).start()

                project(R, xin(m), q(m), m)
                key = lax.broadcasted_iota(jnp.int32, (enc_keys, PAIR), 0)
                seen = (key < sl[m]) | ((key >= R) & (key < R + PRE))
                bias[...] = jnp.where(seen, 0.0, NEG)
                attend(
                    ENC_PAIRS, R, R, True, pairs, q(m), k.at[m], tt, vtp, lambda p: pw.at[m, p], bias, ot,
                )

                @pl.when(m == 0)
                def _():
                    for b in (3, 16, 17):
                        fetch(b).wait()

                f1[...] = xin(m)[...].astype(F32) + dot(ot[...].T, w[3])

                def norm(r):
                    shaped, factor = norm_of(f1[r])
                    xh1[m, r] = shaped.astype(BF)
                    r1[m, r] = factor
                    h = shaped * gain(0)
                    f1[r] = h
                    yb(m)[r] = h.astype(BF)

                by_rows(R, norm)
                branch(ENC_CHUNKS, R, yb(m), slope(m), m)


                @pl.when(m == 1)
                def _():
                    for i in range(src_rows // PAIR):
                        memory_copy(0, i).wait_send()

                def last(r):
                    shaped, factor = norm_of(f1[r])
                    xh2[m, r] = shaped.astype(BF)
                    r2[m, r] = factor
                    snd[r] = (shaped * gain(1)).astype(BF)
                    memory_copy(m, r.start // PAIR).start()

                by_rows(R, last)

            def backward(m):

                @pl.when(m == 0)
                def _():
                    for i in range(src_rows // PAIR):
                        memory_copy(1, i).wait_send()

                back_copy(m, 0).wait_recv()
                back_copy(m, 1).wait_recv()

                def norm(r):
                    dt = norm_back(rcv[m, r].astype(F32), xh2[m, r].astype(F32), r2[m, r], gain(1))
                    f1[r] = dt
                    df(m)[r] = dt.astype(BF)

                by_rows(R, norm)
                g = w.at[12]

                @pl.when(m == 1)
                def _():
                    write_out(ENC_GRADS, g, lambda: w[14, 512 : 512 + 2 * R], 2 * R)
                    start("B", 0, g)

                branch_back_adapter(R, df(m), m)

                @pl.when(m == 1)
                def _():
                    write_in(ENC_GRADS, g, lambda r: w[14, 0 : 2 * R, r], 2 * R)
                    start("A", 0, g)

                branch_back_feed(ENC_CHUNKS, R, df(m), slope(m), m, False)

                def between():
                    @pl.when(m == 1)
                    def _():
                        finish_both(0, g)

                self_back(ENC_PAIRS, R, m, q(m), between)

                @pl.when(m == 1)
                def _():
                    small_begin()
                    finish_stage("B", 1, g)

                self_input(R, xin(m))

                @pl.when(m == 1)
                def _():
                    small_middle()
                    finish_stage("A", 1, g)

                store_x(m).start()

            def store_x(m):
                return pltpu.make_async_copy(xin(m), tok.at[0, m], osem.at[m])

            prefix_setup(R)
            twice(forward)
            twice(backward)
            small_late()
            finish_both(2, w.at[12])
            store_x(0).wait()
            store_x(1).wait()
            small_finish()

        def decoder():
            R = tgt_rows

            def pick(c):
                parts = [pw[1, 2 * c + i // 2, pl.ds((i % 2) * R, R), 256:512] for i in range(4)]
                return jnp.concatenate(parts, axis=1)

            def put(c, value):
                for i in range(4):
                    pw[1, 2 * c + i // 2, pl.ds((i % 2) * R, R), 256:512] = value[:, 256 * i : 256 * (i + 1)]

            slope = (pick, put)

            def dq_(m):
                return k.at[m, pl.ds(dec_keys, R)]

            def dqc_(m):
                return v.at[m, pl.ds(dec_keys, R)]

            def self_probs(m):
                return lambda p: pw.at[m, p, pl.ds(0, dec_keys), pl.ds(0, 2 * R)]

            def cross_probs():
                return lambda p: pw.at[0, p, pl.ds(0, src_rows), pl.ds(2 * R, 2 * R)]

            def self_forward():
                load_t(0).wait()
                load_t(1).wait()
                fetch(0).wait()
                for b in (3, 12, 4, 5, 6, 7):
                    fetch(b).start()
                rows = dxin[...].reshape(2 * R, features)
                queries = (dot(rows, w[0]) * 0.125).astype(BF)
                fetch(1).wait()
                keys = dot(rows, w[1]).astype(BF)
                fetch(2).wait()
                for b in (13, 14, 15, 16, 17, 8, 9, 10, 11):
                    fetch(b).start()
                load_c(0).start()
                load_c(1).start()
                values = dot(rows, w[2]).astype(BF)
                for m in range(2):
                    own = slice(m * R, (m + 1) * R)
                    dq_(m)[...] = queries[own]
                    k[m, 0:R] = keys[own]
                    kt[m, :, 0:R] = keys[own].T
                    v[m, 0:R] = values[own]
                tt[...] = values.T
                key = lax.broadcasted_iota(jnp.int32, (dec_keys, PAIR), 0)
                query = lax.broadcasted_iota(jnp.int32, (dec_keys, PAIR), 1)
                seen = (key <= query) | ((key >= R) & (key < R + PRE))
                bias[0:dec_keys] = jnp.where(seen, 0.0, NEG)

                def mix(m):
                    attend(
                        SELF_PAIRS, R, R, True, pairs, dq_(m), k.at[m, pl.ds(0, dec_keys)],
                        tt.at[:, rows_of(m * R, R)], vtp, self_probs(m), bias.at[pl.ds(0, dec_keys)],
                        ot.at[:, rows_of(m * R, R)],
                    )

                twice(mix)
                fetch(3).wait()
                f1[...] = dxin[...].reshape(2 * R, features).astype(F32) + dot(ot[...].T, w[3])

                def norm(m):
                    shaped, factor = norm_of(f1[rows_of(m * R, R)])
                    xh1[m, 0:R] = shaped.astype(BF)
                    r1[m, 0:R] = factor
                    h = shaped * gain(0)
                    da[m] = h
                    xh1[m, R : 2 * R] = h.astype(BF)

                twice(norm)
                fetch(12).wait()
                crossed = (dot(xh1[:, R : 2 * R].reshape(2 * R, features), w[12]) * 0.125).astype(BF)
                for m in range(2):
                    dqc_(m)[...] = crossed[m * R : (m + 1) * R]

            def self_backward(g):
                sides = jnp.concatenate([kt[m, :, R : 2 * R].T for m in range(2)], axis=0)
                f1[...] = da[...].reshape(2 * R, features) + dot_t(sides, w[12])

                def norm(m):
                    r = rows_of(m * R, R)
                    dt = norm_back(f1[r], xh1[m, 0:R].astype(F32), r1[m, 0:R], gain(0))
                    f1[r] = dt
                    dqkv[0, r] = dt.astype(BF)

                for b in range(4):
                    fetch(b).wait()
                twice(norm)
                dqkv[0] = dot_t(dqkv[0], w[3]).astype(BF)
                finish_both(0, g)

                def unmix(m):
                    r = rows_of(m * R, R)
                    attend_back(
                        SELF_PAIRS, R, R, True, pairs, dqkv.at[0, r], dq_(m),
                        k.at[m, pl.ds(0, dec_keys)], v.at[m, pl.ds(0, dec_keys)],
                        kt.at[m, :, pl.ds(0, R)], ktp, self_probs(m),
                        ot.at[:, r], dqkv.at[1, r], dqkv.at[2, r], pre_sum,
                    )

                twice(unmix)
                dqkv[0] = ot[...].T
                small_begin()
                finish_both(1, g)
                total = f1[...]
                for b in range(3):
                    total = total + dot_t(dqkv[b], w[b])
                low = total.astype(BF)
                for m in range(2):
                    dxin[m] = low[m * R : (m + 1) * R]
                    store_y(m).start()

            def middle(m):
                @pl.when(m == 0)
                def _():
                    for b in (13, 14, 15, 16, 17, 8, 9, 10, 11):
                        fetch(b).wait()
                    load_c(0).wait()
                    load_c(1).wait()

                for i in range(src_rows // PAIR):
                    memory_copy(m, i).wait_recv()

                keys = dot(rcv[m], w[13]).astype(BF)
                kc[...] = keys
                kct[...] = keys.T
                values = dot(rcv[m], w[14]).astype(BF)
                vc[...] = values
                tt[...] = values.T
                key = lax.broadcasted_iota(jnp.int32, (src_rows, PAIR), 0)
                bias[0:src_rows] = jnp.where(key < sl[m], 0.0, NEG)
                attend(
                    CROSS_PAIRS, R, src_rows, False, pairs, dqc_(m), kc, tt, None, cross_probs(),
                    bias.at[pl.ds(0, src_rows)], ot.at[:, pl.ds(0, R)],
                )
                f1[0:R] = da[m] + dot(ot[:, 0:R].T, w[15])
                yb = xh1.at[m, pl.ds(R, R)]

                def norm(r):
                    shaped, factor = norm_of(f1[r])
                    xh2[m, r] = shaped.astype(BF)
                    r2[m, r] = factor
                    h = shaped * gain(1)
                    f1[r] = h
                    yb[r] = h.astype(BF)

                by_rows(R, norm)
                branch(DEC_CHUNKS, R, yb, slope, m)
                df = xh2.at[m, pl.ds(R, R)]

                def turn(r):
                    shaped, factor = norm_of(f1[r])
                    row = lax.broadcasted_iota(jnp.int32, (LN_ROWS, 1), 0) + r.start
                    on = jnp.where(row < tl[m], 1.0, 0.0)
                    grad = dct[m, r].astype(F32) * on
                    dct[m, r] = (shaped * gain(2) * on).astype(BF)
                    dt = norm_back(grad, shaped, factor, gain(2))
                    f1[r] = dt
                    df[r] = dt.astype(BF)

                by_rows(R, turn)
                store_d(m).start()
                branch_back_adapter(R, df, m)
                branch_back_feed(DEC_CHUNKS, R, df, slope, m, True)

                @pl.when(m == 1)
                def _():
                    back_copy(0, 0).wait_send()
                    back_copy(0, 1).wait_send()
                    for b in range(4):
                        fetch(b).start()
                    write_out(DEC_GRADS, g, lambda: xh2[:, R : 2 * R].reshape(2 * R, features), 2 * R)
                    start("B", 0, g)
                    write_in(DEC_GRADS, g, lambda r: xh1[:, R : 2 * R, r].reshape(2 * R, 2 * PAIR), 2 * R)
                    start("A", 0, g)

                def back(r):
                    dt = norm_back(f1[r], xh2[m, r].astype(F32), r2[m, r], gain(1))
                    f1[r] = dt
                    dqkv[0, r] = dt.astype(BF)

                by_rows(R, back)
                grad_mixed = dot_t(dqkv[0, 0:R], w[15]).astype(BF)
                dqkv[0, 0:R] = grad_mixed
                attend_back(
                    CROSS_PAIRS, R, src_rows, False, pairs, dqkv.at[0, pl.ds(0, R)], dqc_(m), kc, vc, kct, None,
                    cross_probs(), kt.at[m, :, pl.ds(R, R)], dqkv.at[1], dqkv.at[2], None,
                )

                span = features // 2
                for i in range(2):
                    part = pl.ds(i * span, span)
                    snd[:, part] = (dot_t(dqkv[1], w[13, part]) + dot_t(dqkv[2], w[14, part])).astype(BF)
                    back_copy(m, i).start()
                da[m] = f1[0:R]

            def store_d(m):
                return pltpu.make_async_copy(dct.at[m], tok.at[0, m, pl.ds(0, R)], osem.at[m])

            def store_y(m):
                return pltpu.make_async_copy(dxin.at[m], tok.at[0, m, pl.ds(R, R)], osem.at[2 + m])

            g = w.at[8]
            prefix_setup(R)
            self_forward()

            def turn_block(c, carry):
                fetch_in(c).wait()
                w[c] = w[4 + c].T
                return carry

            lax.fori_loop(0, chunks, turn_block, 0)
            twice(middle)
            self_backward(g)
            small_middle()
            finish_both(2, g)
            small_late()
            for m in range(2):
                store_d(m).wait()
                store_y(m).wait()
            back_copy(1, 0).wait_send()
            back_copy(1, 1).wait_send()
            small_finish()

        @pl.when(section == 0)
        def _():
            encoder_loads()

        @pl.when(section == 1)
        def _():
            decoder_loads()

        greet()
        pl.when(section == 0)(encoder)
        pl.when(section == 1)(decoder)

    vm = pltpu.VMEM
    plane = nx * ny
    piece = small_rows * features // (16 * plane)
    smalls = 2 * (plane - 1) + nz - 1
    scratch = [
        vm((16, features, features), BF),
        vm((features, adapt), BF),
        vm((adapt, features), BF),
        vm((2, pairs, enc_keys, 2 * src_rows), BF),
        vm((2, enc_keys, features), BF),
        vm((2, enc_keys, features), BF),
        vm((2, features, src_rows), BF),
        vm((features, src_rows), BF),
        vm((features, src_rows), BF),
        vm((features, PRE_PAD), BF),
        vm((features, PRE_PAD), BF),
        vm((2, src_rows, features), BF),
        vm((2, src_rows, features), BF),
        vm((2, src_rows, 1), F32),
        vm((2, src_rows, 1), F32),
        vm((2, src_rows, adapt), BF),
        vm((2 * src_rows, adapt), BF),
        vm((2 * src_rows, adapt), BF),
        vm((src_rows, features), BF),
        vm((2, src_rows, features), BF),
        vm((src_rows, features), F32),
        vm((3, src_rows, features), BF),
        vm((nx - 1, ny * nz * ra, adapt), BF),
        vm((ny - 1, nz * ra, adapt), BF),
        vm((nz - 1, ra, adapt), BF),
        vm((ny - 1, nx * nz * ra, adapt), BF),
        vm((nx - 1, nz * ra, adapt), BF),
        vm((nz - 1, ra, adapt), BF),
        vm((2, PRE_PAD, features), F32),
        vm((enc_keys, PAIR), F32),
        vm((1, adapt), F32),
        vm((1, features), F32),
        vm((small_rows, features), BF),
        vm((plane - 1, 16, piece), BF),
        vm((16, piece), BF),
        vm((nz - 1, 16, piece), BF),
        vm((16, piece), BF),
        vm((small_rows, features), BF),
        vm((2, tgt_rows, features), BF),
        vm((2, tgt_rows, features), BF),
        vm((2, tgt_rows, features), F32),
        vm((src_rows, features), BF),
        vm((src_rows, features), BF),
        vm((features, src_rows), BF),
        pltpu.SemaphoreType.DMA((18,)),
        pltpu.SemaphoreType.DMA((4,)),
        pltpu.SemaphoreType.DMA((4,)),
        pltpu.SemaphoreType.DMA((4,)),
        pltpu.SemaphoreType.DMA((4,)),
        pltpu.SemaphoreType.DMA((18,)),
        pltpu.SemaphoreType.DMA((18,)),
        pltpu.SemaphoreType.DMA((smalls,)),
        pltpu.SemaphoreType.DMA((smalls,)),
    ]
    return kernel, scratch, ra


def finish(tok, ig_in, og_in, small_in, tok_out, pre_out, ig_out, og_out, ib_out, ob_out, held, ig, og, small, sem):
    micro = tok.shape[1]
    loads = [pltpu.make_async_copy(tok.at[0, m], held.at[0, m], sem.at[m]) for m in range(micro)]
    stores = [pltpu.make_async_copy(held.at[0, m], tok_out.at[0, m], sem.at[micro + m]) for m in range(micro)]
    rest = [(small_in, small, 4), (ig_in, ig, 5), (og_in, og, 6)]
    rest = [pltpu.make_async_copy(a, b, sem.at[i]) for a, b, i in rest]
    for copy in loads + rest:
        copy.start()
    for load, store in zip(loads, stores):
        load.wait()
        store.start()
    for copy in rest:
        copy.wait()
    adapt = ig.shape[1]
    pre_out[:, 0, :] = small[0:PRE]
    pre_out[:, 1, :] = small[PRE_PAD : PRE_PAD + PRE]
    ig_out[0] = ig[...]
    og_out[0] = og[...]
    ob_out[...] = small[PRE : PRE + 1]
    ib_out[...] = small[PRE_PAD + PRE : PRE_PAD + PRE + 1, 0:adapt]
    for store in stores:
        store.wait()


def solution(mesh):
    dp = mesh.shape["dp"]
    nz = 4
    nx = math.isqrt(dp // nz)
    ny = dp // (nz * nx)

    def per_device(
        source, target, cotangent, source_lengths, target_lengths, attention_in, attention_out,
        cross_query, cross_pair, cross_output, feed_in, feed_out, adapter_in, adapter_in_bias,
        adapter_out, adapter_out_bias, prefix, norm_gains,
    ):
        features = source.shape[2]
        adapt = adapter_in.shape[2]
        kernel, scratch, ra = make_kernel(
            nz, ny, nx, features, feed_in.shape[2], adapt, source.shape[1], target.shape[1]
        )
        anywhere = pl.BlockSpec(memory_space=pl.ANY)
        scalar = pl.BlockSpec(memory_space=pltpu.SMEM)
        vector = pl.BlockSpec(memory_space=pltpu.VMEM)
        tok, ig, og, small = pl.pallas_call(
            kernel,
            out_shape=(
                jax.ShapeDtypeStruct((1, source.shape[0], source.shape[1], features), BF),
                jax.ShapeDtypeStruct((ra, adapt), F32),
                jax.ShapeDtypeStruct((ra // 2, features), F32),
                jax.ShapeDtypeStruct((2 * PRE_PAD, features), F32),
            ),
            in_specs=[anywhere] * 3 + [scalar] * 2 + [anywhere] * 9 + [vector] * 4,
            out_specs=(anywhere, vector, vector, vector),
            scratch_shapes=scratch,
            compiler_params=pltpu.CompilerParams(
                collective_id=0, has_side_effects=True, vmem_limit_bytes=67000000
            ),
        )(
            source, target, cotangent, source_lengths.reshape(-1), target_lengths.reshape(-1), attention_in,
            attention_out, cross_query, cross_pair, cross_output, feed_in, feed_out, adapter_in, adapter_out,
            adapter_in_bias, adapter_out_bias, prefix[0].transpose(1, 0, 2), norm_gains,
        )
        tok, pre, ig, og, ib, ob = pl.pallas_call(
            finish,
            out_shape=(
                jax.ShapeDtypeStruct(tok.shape, BF),
                jax.ShapeDtypeStruct((PRE, 2, features), F32),
                jax.ShapeDtypeStruct((1, ra, adapt), F32),
                jax.ShapeDtypeStruct((1, ra // 2, features), F32),
                jax.ShapeDtypeStruct((1, adapt), F32),
                jax.ShapeDtypeStruct((1, features), F32),
            ),
            in_specs=[anywhere, anywhere, anywhere, anywhere],
            out_specs=(anywhere, vector, vector, vector, vector, vector),
            scratch_shapes=[
                pltpu.VMEM(tok.shape, BF),
                pltpu.VMEM(ig.shape, F32),
                pltpu.VMEM(og.shape, F32),
                pltpu.VMEM(small.shape, F32),
                pltpu.SemaphoreType.DMA((7,)),
            ],
        )(tok, ig, og, small)
        return tok, pre.transpose(1, 0, 2)[None], ig, og, ib, ob

    return jax.shard_map(
        per_device,
        mesh=mesh,
        in_specs=(
            P(None, "dp", None),
            P(None, "dp", None),
            P(None, "dp", None),
            P(None, "dp"),
            P(None, "dp"),
            P("section", None, None),
            P("section", None, None),
            P(),
            P(),
            P(),
            P("section", None, None),
            P("section", None, None),
            P("section", None, None),
            P("section", None),
            P("section", None, None),
            P("section", None),
            P("section", None, None, None),
            P("section", None, None),
        ),
        out_specs=(
            P("section", None, "dp", None),
            P("section", None, None, None),
            P("section", "dp", None),
            P("section", "dp", None),
            P("section", None),
            P("section", None),
        ),
        check_vma=False,
    )
```

```python
import math

import jax
import jax.numpy as jnp
from jax import lax
from jax.experimental import pallas as pl
from jax.experimental.pallas import tpu as pltpu
from jax.sharding import PartitionSpec as P

BF = jnp.bfloat16
F32 = jnp.float32
MESH = pl.DeviceIdType.MESH
EPS = 1e-05
NEG = -1e30
ROOT_HALF = 0.7071067811865476
INV_ROOT_TWO_PI = 0.3989422804014327
PRE = 30
PRE_PAD = 32
PAIR = 128
HALF = 64
LN_ROWS = 128
ENC_PAIRS = 8
SELF_PAIRS = 2
CROSS_PAIRS = 8
ENC_CHUNKS = 1
DEC_CHUNKS = 4
TURNED = 1
ENC_GRADS = 1
DEC_GRADS = 4


def dot(a, b):
    return jnp.dot(a, b, preferred_element_type=F32)


def dot_t(a, b):
    return lax.dot_general(a, b, (((1,), (1,)), ((), ())), preferred_element_type=F32)


def tdot(a, b):
    return lax.dot_general(a, b, (((0,), (0,)), ((), ())), preferred_element_type=F32)


def gelu_and_slope(v):
    cdf = 0.5 + 0.5 * lax.erf(v * ROOT_HALF)
    return v * cdf, cdf + v * (jnp.exp(-0.5 * v * v) * INV_ROOT_TWO_PI)


def rows_of(start, count):
    return pl.ds(pl.multiple_of(start, count), count)


def by_rows(count, body):
    def step(i, carry):
        body(rows_of(i * LN_ROWS, LN_ROWS))
        return carry

    lax.fori_loop(0, count // LN_ROWS, step, 0)


def norm_of(total):
    centre = total - jnp.mean(total, axis=-1, keepdims=True)
    factor = lax.rsqrt(jnp.mean(centre * centre, axis=-1, keepdims=True) + EPS)
    return centre * factor, factor


def norm_back(grad, shaped, factor, gain):
    scaled = grad * gain
    centred = scaled - jnp.mean(scaled, axis=-1, keepdims=True)
    return factor * (centred - shaped * jnp.mean(scaled * shaped, axis=-1, keepdims=True))


def both_heads(block):
    first = lax.broadcasted_iota(jnp.int32, block.shape, 1) < HALF
    zero = jnp.zeros_like(block)
    return jnp.concatenate([jnp.where(first, block, zero), jnp.where(first, zero, block)], axis=0)


def attend(unroll, rows, tokens, prefixed, pairs, q, k, vt, vtp, probs, bias, out_t):
    def step(p, carry):
        lanes = rows_of(p * PAIR, PAIR)
        scores = dot_t(k[:, lanes], both_heads(q[:, lanes]))
        shift = bias[...]
        scores = scores + jnp.concatenate([shift] * (2 * rows // PAIR), axis=1)
        power = jnp.exp(scores - jnp.max(scores, axis=0, keepdims=True))
        low = (power * (1.0 / jnp.sum(power, axis=0, keepdims=True))).astype(BF)
        probs(p)[...] = low
        for a in range(2):
            head = rows_of(p * PAIR + a * HALF, HALF)
            part = low[:, a * rows : (a + 1) * rows]
            mixed = dot(vt[head, :], part[:tokens])
            if prefixed:
                mixed = mixed + dot(vtp[head, :], part[tokens:])
            out_t[head, :] = mixed.astype(BF)
        return carry

    lax.fori_loop(0, pairs, step, 0, unroll=unroll)


def attend_back(unroll, rows, tokens, prefixed, pairs, grad, q, v, kt, ktp, probs, dq_t, dk, dv, pre_sum):
    def step(p, carry):
        lanes = rows_of(p * PAIR, PAIR)
        grads = both_heads(grad[:, lanes])
        queries = both_heads(q[:, lanes])
        low = probs(p)[...]
        wide = low.astype(F32)
        grad_probs = dot_t(v[:, lanes], grads)
        inner = jnp.sum(wide * grad_probs, axis=0, keepdims=True)
        grad_scores = (wide * (grad_probs - inner)).astype(BF)
        grad_keys = dot(grad_scores, queries)
        grad_values = dot(low, grads)
        dk[:, lanes] = grad_keys[:tokens].astype(BF)
        dv[:, lanes] = grad_values[:tokens].astype(BF)
        if prefixed:
            pre_sum[0, :, lanes] = pre_sum[0, :, lanes] + grad_keys[tokens:]
            pre_sum[1, :, lanes] = pre_sum[1, :, lanes] + grad_values[tokens:]
        for a in range(2):
            head = rows_of(p * PAIR + a * HALF, HALF)
            part = grad_scores[:, a * rows : (a + 1) * rows]
            back = dot(kt[head, :], part[:tokens])
            if prefixed:
                back = back + dot(ktp[head, :], part[tokens:])
            dq_t[head, :] = (back * 0.125).astype(BF)
        return carry

    lax.fori_loop(0, pairs, step, 0, unroll=unroll)


def make_kernel(nz, ny, nx, features, hidden, adapt, src_rows, tgt_rows):
    chunks = hidden // features
    pairs = features // PAIR
    dp = nz * ny * nx
    ra = features // dp
    enc_keys = src_rows + PRE_PAD
    dec_keys = tgt_rows + PRE_PAD
    small_rows = 2 * PRE_PAD

    def kernel(
        src, tgt, ct, sl, tl, ai, ao, cq, cp, co, fi, fo, di, do, bi, bo, prefix, gains,
        tok, ig_out, og_out, sm_out,
        w, wdi, wdo, pw, k, v, kt, tt, ot, ktp, vtp, xh1, xh2, rr, sa, rb, dz, snd, rcv,
        f1, dqkv, rsx, rsy, rsz, rsa, rsb, rsc, pre_sum, bias, ib_sum, ob_sum,
        small, small_in, small_mid, small_z, small_end, small_all,
        dxin, dct, da, vc, kct,
        wsem, xsem, osem, ssem, rsem, gss, grs, mss, mrs,
    ):
        section = lax.axis_index("section")
        here = lax.axis_index("dp")
        at = {"x": lax.rem(here, nx), "y": lax.rem(here // nx, ny), "z": here // (nx * ny)}
        size = {"x": nx, "y": ny, "z": nz}

        def peer(axis, step):
            c = dict(at)
            c[axis] = lax.rem(at[axis] + step, size[axis])
            return c[axis], (section, (c["z"] * ny + c["y"]) * nx + c["x"])

        other = (1 - section, here)
        def remote(source, target, send, receive, device):
            return pltpu.make_async_remote_copy(
                src_ref=source, dst_ref=target, send_sem=send, recv_sem=receive,
                device_id=device, device_id_type=MESH,
            )

        def memory_copy(m, i):
            rows = rows_of(i * PAIR, PAIR)
            return remote(snd.at[rows], rcv.at[m, rows], ssem.at[2 * m + i], rsem.at[2 * m + i], other)

        def back_copy(m, i):
            lanes = pl.ds(i * (features // 2), features // 2)
            return remote(snd.at[:, lanes], rcv.at[m, :, lanes], ssem.at[2 * m + i], rsem.at[2 * m + i], other)

        def greet():
            barrier = pltpu.get_barrier_semaphore()
            partners = [other] + [peer("z", s)[1] for s in range(1, nz)]
            for s in range(1, nx * ny):
                partners.append((section, at["z"] * nx * ny + lax.rem(at["y"] * nx + at["x"] + s, nx * ny)))
            for partner in partners:
                pl.semaphore_signal(barrier, inc=1, device_id=partner, device_id_type=MESH)
            pl.semaphore_wait(barrier, len(partners))

        widths = {"x": nx, "y": ny, "z": nz}
        orders = {"A": "xyz", "B": "yxz"}
        landing = {"A": (rsx, rsy, rsz), "B": (rsa, rsb, rsc)}

        def reduce_phase(part, stage, g):
            axis = orders[part][stage]
            count = ra
            for later in orders[part][stage + 1 :]:
                count *= size[later]
            lanes = slice(0, adapt) if part == "A" else slice(adapt, 2 * adapt)
            copies = []
            base = 0 if part == "A" else 9
            for s in range(1, size[axis]):
                c, device = peer(axis, s)
                rows = rows_of(c * count, count)
                source = g.at[rows, lanes] if stage == 0 else landing[part][stage - 1].at[0, rows]
                i = base + 3 * stage + s - 1
                copies.append(remote(source, landing[part][stage].at[s - 1], gss.at[i], grs.at[i], device))
            return copies

        def reduce_sum(part, stage, g):
            axis = orders[part][stage]
            count = ra
            for later in orders[part][stage + 1 :]:
                count *= size[later]
            lanes = slice(0, adapt) if part == "A" else slice(adapt, 2 * adapt)
            rows = rows_of(at[axis] * count, count)
            mine = g[rows, lanes] if stage == 0 else landing[part][stage - 1][0, rows]
            total = mine.astype(F32)
            for s in range(size[axis] - 1):
                total = total + landing[part][stage][s].astype(F32)
            return total

        def place(d, part):
            z, y, x = lax.div(d, nx * ny), lax.rem(lax.div(d, nx), ny), lax.rem(d, nx)
            if part == "A":
                return pl.multiple_of(((x * ny + y) * nz + z) * ra, ra)
            return pl.multiple_of(((y * nx + x) * nz + z) * ra, ra)

        def write_in(unroll, g, ybs, count):
            group = 2 * PAIR

            def step(t, carry):
                block = tdot(ybs(rows_of(t * group, group)), dz[0:count])
                for i in range(group // ra):
                    d = t * (group // ra) + i
                    g[pl.ds(place(d, "A"), ra), 0:adapt] = block[i * ra : (i + 1) * ra].astype(BF)
                return carry

            lax.fori_loop(0, features // group, step, 0, unroll=unroll)

        def write_out(unroll, g, dfs, count):
            half = ra // 2

            def step(t, carry):
                block = 4.0 * tdot(rb[0:count, rows_of(t * PAIR, PAIR)], dfs())
                for i in range(PAIR // half):
                    d = t * (PAIR // half) + i
                    part = block[i * half : (i + 1) * half]
                    part = jnp.concatenate([part[:, :adapt], part[:, adapt:]], axis=0)
                    g[pl.ds(place(d, "B"), ra), adapt : 2 * adapt] = part.astype(BF)
                return carry

            lax.fori_loop(0, adapt // PAIR, step, 0, unroll=unroll)

        def start(part, stage, g):
            for c in reduce_phase(part, stage, g):
                c.start()

        def finish_stage(part, stage, g):
            for c in reduce_phase(part, stage, g):
                c.wait()
            total = reduce_sum(part, stage, g)
            if stage < 2:
                landing[part][stage][0] = total.astype(BF)
                start(part, stage + 1, g)
            elif part == "A":
                ig_out[...] = total
            else:
                half = ra // 2
                og_out[:, 0:adapt] = total[:half]
                og_out[:, adapt : 2 * adapt] = total[half:]

        def finish_both(stage, g):
            finish_stage("B", stage, g)
            finish_stage("A", stage, g)

        plane = nx * ny
        piece = small_rows * features // (16 * plane)
        across = features // piece
        seat = at["y"] * nx + at["x"]

        def plane_peer(s):
            i = lax.rem(seat + s, plane)
            return i, (section, at["z"] * plane + i)

        def small_at(ref, i):
            return ref.at[rows_of((i // across) * 16, 16), rows_of(lax.rem(i, across) * piece, piece)]

        def small_scatter():
            copies = []
            for s in range(1, plane):
                i, device = plane_peer(s)
                copies.append(remote(small_at(small, i), small_in.at[s - 1], mss.at[s - 1], mrs.at[s - 1], device))
            return copies

        def small_along():
            n = plane - 1
            return [
                remote(small_mid, small_z.at[s - 1], mss.at[n + s - 1], mrs.at[n + s - 1], peer("z", s)[1])
                for s in range(1, nz)
            ]

        def small_gather():
            n = plane - 1 + nz - 1
            copies = []
            for s in range(1, plane):
                device = plane_peer(s)[1]
                copies.append(
                    remote(small_end, small_at(small_all, seat), mss.at[n + s - 1], mrs.at[n + s - 1], device)
                )
            return copies

        def small_begin():
            small[0:PRE_PAD] = pre_sum[0].astype(BF)
            small[PRE_PAD : 2 * PRE_PAD] = pre_sum[1].astype(BF)
            small[PRE : PRE + 1] = ob_sum[...].astype(BF)
            small[PRE_PAD + PRE : PRE_PAD + PRE + 1, 0:adapt] = ib_sum[...].astype(BF)
            for c in small_scatter():
                c.start()

        def small_middle():
            for c in small_scatter():
                c.wait()
            total = small_at(small, seat)[...].astype(F32)
            for s in range(plane - 1):
                total = total + small_in[s].astype(F32)
            small_mid[...] = total.astype(BF)
            for c in small_along():
                c.start()

        def small_late():
            for c in small_along():
                c.wait()
            total = small_mid[...].astype(F32)
            for s in range(nz - 1):
                total = total + small_z[s].astype(F32)
            small_end[...] = total.astype(BF)
            small_at(small_all, seat)[...] = small_end[...]
            for c in small_gather():
                c.start()

        def small_finish():
            for c in small_gather():
                c.wait()
            sm_out[...] = small_all[...].astype(F32)

        blocks = {}
        for b in range(3):
            blocks[b] = (ai.at[0, :, pl.ds(b * features, features)], w.at[b])
        blocks[3] = (ao.at[0], w.at[3])
        for c in range(chunks):
            blocks[4 + c] = (fi.at[0, :, pl.ds(c * features, features)], w.at[4 + c])
            blocks[8 + c] = (fo.at[0, pl.ds(c * features, features), :], w.at[8 + c])
        blocks[12] = (cq, w.at[12])
        blocks[13] = (cp.at[:, pl.ds(0, features)], w.at[13])
        blocks[14] = (cp.at[:, pl.ds(features, features)], w.at[14])
        blocks[15] = (co, w.at[15])
        blocks[16] = (di.at[0], wdi)
        blocks[17] = (do.at[0], wdo)

        def fetch_in(c):
            lanes = rows_of(c * features, features)
            return pltpu.make_async_copy(fi.at[0, :, lanes], w.at[4 + c], wsem.at[4 + c])

        def fetch_out(c):
            rows = rows_of(c * features, features)
            return pltpu.make_async_copy(fo.at[0, rows, :], w.at[8 + c], wsem.at[8 + c])

        def fetch(b):
            return pltpu.make_async_copy(blocks[b][0], blocks[b][1], wsem.at[b])

        def gain(i):
            return gains[0, i : i + 1, :].astype(F32)

        def prefix_setup(tokens):
            pad = jnp.zeros((PRE_PAD, features), BF)
            for m in range(2):
                k[m, pl.ds(tokens, PRE_PAD)] = pad
                v[m, pl.ds(tokens, PRE_PAD)] = pad
                k[m, pl.ds(tokens, PRE)] = prefix[:, 0, :]
                v[m, pl.ds(tokens, PRE)] = prefix[:, 1, :]
            ktp[...] = k[0, pl.ds(tokens, PRE_PAD)].T
            vtp[...] = v[0, pl.ds(tokens, PRE_PAD)].T
            pre_sum[...] = jnp.zeros_like(pre_sum)
            ib_sum[...] = jnp.zeros_like(ib_sum)
            ob_sum[...] = jnp.zeros_like(ob_sum)

        def project(rows, x, q, m):
            q[...] = (dot(x[...], w[0]) * 0.125).astype(BF)
            keys = dot(x[...], w[1]).astype(BF)
            k[m, 0:rows] = keys
            kt[m, :, 0:rows] = keys.T
            values = dot(x[...], w[2]).astype(BF)
            v[m, 0:rows] = values
            tt[:, 0:rows] = values.T

        def branch(unroll, rows, yb, slope, m):
            pre = dot(yb[...], wdi[...]) + bi[...].astype(F32)
            act, turn = gelu_and_slope(pre)
            act = act.astype(BF)
            rb[rows_of(m * rows, rows)] = act
            sa[m, 0:rows] = turn.astype(BF)
            f1[0:rows] = f1[0:rows] + 4.0 * (dot(act, wdo[...]) + bo[...].astype(F32))

            if rows == src_rows:

                @pl.when(m == 0)
                def _():
                    for b in (4, 8, 5, 9, 6, 10, 7, 11):
                        fetch(b).wait()

            def step(c, carry):
                act, turn = gelu_and_slope(dot(yb[...], w[4 + c]))
                slope[1](c, turn.astype(BF))
                f1[0:rows] = f1[0:rows] + dot(act.astype(BF), w[8 + c])
                return carry

            lax.fori_loop(0, chunks, step, 0, unroll=unroll)

        def branch_back_adapter(rows, df, m):
            low = df[...]
            ob_sum[...] = ob_sum[...] + 4.0 * jnp.sum(low.astype(F32), axis=0, keepdims=True)
            grad = ((4.0 * dot_t(low, wdo[...])) * sa[m, 0:rows].astype(F32)).astype(BF)
            dz[rows_of(m * rows, rows)] = grad
            ib_sum[...] = ib_sum[...] + jnp.sum(grad.astype(F32), axis=0, keepdims=True)

        def branch_back_feed(unroll, rows, df, slope, m, turned):
            f1[0:rows] = f1[0:rows] + dot_t(dz[rows_of(m * rows, rows)], wdi[...])

            def step(c, carry):
                if turned and c < TURNED:
                    grad = dot(df[...], w[16 + c])
                else:
                    grad = dot_t(df[...], w[8 + c])
                grad = (grad * slope[0](c).astype(F32)).astype(BF)
                back = dot(grad, w[c]) if turned else dot_t(grad, w[4 + c])
                f1[0:rows] = f1[0:rows] + back
                return carry

            if turned:
                for c in range(chunks):
                    step(c, 0)
            else:
                lax.fori_loop(0, chunks, step, 0, unroll=unroll)

        def self_back(unroll, rows, m, q, between=None):
            def norm(r):
                dt = norm_back(f1[r], xh1[m, r].astype(F32), rr[m, r, 0:1], gain(0))
                f1[r] = dt
                dqkv[0, r] = dt.astype(BF)

            by_rows(rows, norm)
            ot_rows = dot_t(dqkv[0, 0:rows], w[3]).astype(BF)
            dqkv[0, 0:rows] = ot_rows
            if between is not None:
                between()
            attend_back(
                unroll, rows, rows, True, pairs, dqkv.at[0, pl.ds(0, rows)], q,
                v.at[m, pl.ds(0, rows + PRE_PAD)],
                kt.at[m, :, pl.ds(0, rows)], ktp,
                lambda p: pw.at[m, p, pl.ds(0, rows + PRE_PAD), pl.ds(0, 2 * rows)],
                ot.at[:, pl.ds(0, rows)], dqkv.at[1, pl.ds(0, rows)], dqkv.at[2, pl.ds(0, rows)], pre_sum,
            )
            dqkv[0, 0:rows] = ot[:, 0:rows].T

        def self_input(rows, out):
            total = f1[0:rows]
            for b in range(3):
                total = total + dot_t(dqkv[b, 0:rows], w[b])
            out[...] = total.astype(BF)

        def twice(body):
            def step(m, carry):
                body(m)
                return carry

            lax.fori_loop(0, 2, step, 0)

        def xin(m):
            return w.at[15, rows_of(512 + m * src_rows, src_rows)]

        def load_x(m):
            return pltpu.make_async_copy(src.at[m], xin(m), xsem.at[m])

        def load_t(m):
            return pltpu.make_async_copy(tgt.at[m], dxin.at[m], xsem.at[m])

        def load_c(m):
            return pltpu.make_async_copy(ct.at[m], dct.at[m], xsem.at[2 + m])

        def encoder_loads():
            load_x(0).start()
            for b in (0, 1, 2):
                fetch(b).start()
            load_x(1).start()

        def decoder_loads():
            load_t(0).start()
            for b in [0, 1, 2]:
                fetch(b).start()
            load_t(1).start()

        def encoder():
            R = src_rows

            def q(m):
                return w.at[15, rows_of(m * R, R)]

            def yb(m):
                return w.at[14, rows_of(m * R, R)]

            def df(m):
                return w.at[14, rows_of(512 + m * R, R)]

            def slope(m):
                def put(c, value):
                    w[12 + m, rows_of(c * R, R)] = value

                return (lambda c: w[12 + m, rows_of(c * R, R)]), put

            def forward(m):
                load_x(m).wait()

                @pl.when(m == 0)
                def _():
                    fetch(0).wait()
                    for b in (3, 16, 17, 4, 8):
                        fetch(b).start()
                    fetch(1).wait()
                    fetch(2).wait()
                    for b in (5, 9, 6, 10, 7, 11):
                        fetch(b).start()

                project(R, xin(m), q(m), m)
                key = lax.broadcasted_iota(jnp.int32, (enc_keys, PAIR), 0)
                seen = (key < sl[m]) | ((key >= R) & (key < R + PRE))
                bias[...] = jnp.where(seen, 0.0, NEG)
                attend(
                    ENC_PAIRS, R, R, True, pairs, q(m), k.at[m], tt, vtp, lambda p: pw.at[m, p], bias, ot,
                )

                @pl.when(m == 0)
                def _():
                    for b in (3, 16, 17):
                        fetch(b).wait()

                f1[...] = xin(m)[...].astype(F32) + dot(ot[...].T, w[3])

                def norm(r):
                    shaped, factor = norm_of(f1[r])
                    xh1[m, r] = shaped.astype(BF)
                    rr[m, r, 0:1] = factor
                    h = shaped * gain(0)
                    f1[r] = h
                    yb(m)[r] = h.astype(BF)

                by_rows(R, norm)
                branch(ENC_CHUNKS, R, yb(m), slope(m), m)


                @pl.when(m == 1)
                def _():
                    for i in range(src_rows // PAIR):
                        memory_copy(0, i).wait_send()

                def last(r):
                    shaped, factor = norm_of(f1[r])
                    xh2[m, r] = shaped.astype(BF)
                    rr[m, r, 1:2] = factor
                    snd[r] = (shaped * gain(1)).astype(BF)
                    memory_copy(m, r.start // PAIR).start()

                by_rows(R, last)

            def backward(m):

                @pl.when(m == 0)
                def _():
                    for i in range(src_rows // PAIR):
                        memory_copy(1, i).wait_send()

                back_copy(m, 0).wait_recv()
                back_copy(m, 1).wait_recv()

                def norm(r):
                    dt = norm_back(rcv[m, r].astype(F32), xh2[m, r].astype(F32), rr[m, r, 1:2], gain(1))
                    f1[r] = dt
                    df(m)[r] = dt.astype(BF)

                by_rows(R, norm)
                g = w.at[12]

                @pl.when(m == 1)
                def _():
                    write_out(ENC_GRADS, g, lambda: w[14, 512 : 512 + 2 * R], 2 * R)
                    start("B", 0, g)

                branch_back_adapter(R, df(m), m)

                @pl.when(m == 1)
                def _():
                    write_in(ENC_GRADS, g, lambda r: w[14, 0 : 2 * R, r], 2 * R)
                    start("A", 0, g)

                branch_back_feed(ENC_CHUNKS, R, df(m), slope(m), m, False)

                def between():
                    @pl.when(m == 1)
                    def _():
                        finish_both(0, g)

                self_back(ENC_PAIRS, R, m, q(m), between)

                @pl.when(m == 1)
                def _():
                    small_begin()
                    finish_stage("B", 1, g)

                self_input(R, xin(m))

                @pl.when(m == 1)
                def _():
                    small_middle()
                    finish_stage("A", 1, g)

                store_x(m).start()

            def store_x(m):
                return pltpu.make_async_copy(xin(m), tok.at[0, m], osem.at[m])

            prefix_setup(R)
            twice(forward)
            twice(backward)
            small_late()
            finish_both(2, w.at[12])
            store_x(0).wait()
            store_x(1).wait()
            small_finish()

        def decoder():
            R = tgt_rows

            def pick(c):
                parts = [pw[1, 2 * c + i // 2, pl.ds((i % 2) * R, R), 256:512] for i in range(4)]
                return jnp.concatenate(parts, axis=1)

            def put(c, value):
                for i in range(4):
                    pw[1, 2 * c + i // 2, pl.ds((i % 2) * R, R), 256:512] = value[:, 256 * i : 256 * (i + 1)]

            slope = (pick, put)

            def dq_(m):
                return k.at[m, pl.ds(dec_keys, R)]

            def dqc_(m):
                return v.at[m, pl.ds(dec_keys, R)]

            def self_probs(m):
                return lambda p: pw.at[m, p, pl.ds(0, dec_keys), pl.ds(0, 2 * R)]

            def cross_probs():
                return lambda p: pw.at[0, p, pl.ds(0, src_rows), pl.ds(2 * R, 2 * R)]

            def self_forward():
                load_t(0).wait()
                load_t(1).wait()
                fetch(0).wait()
                for b in (3, 12, 4, 5, 6, 7):
                    fetch(b).start()
                rows = dxin[...].reshape(2 * R, features)
                queries = (dot(rows, w[0]) * 0.125).astype(BF)
                fetch(1).wait()
                keys = dot(rows, w[1]).astype(BF)
                fetch(2).wait()
                for b in (13, 14, 15, 16, 17, 8, 9, 10, 11):
                    fetch(b).start()
                load_c(0).start()
                load_c(1).start()
                values = dot(rows, w[2]).astype(BF)
                for m in range(2):
                    own = slice(m * R, (m + 1) * R)
                    dq_(m)[...] = queries[own]
                    k[m, 0:R] = keys[own]
                    kt[m, :, 0:R] = keys[own].T
                    v[m, 0:R] = values[own]
                tt[...] = values.T
                key = lax.broadcasted_iota(jnp.int32, (dec_keys, PAIR), 0)
                query = lax.broadcasted_iota(jnp.int32, (dec_keys, PAIR), 1)
                seen = (key <= query) | ((key >= R) & (key < R + PRE))
                bias[0:dec_keys] = jnp.where(seen, 0.0, NEG)

                def mix(m):
                    attend(
                        SELF_PAIRS, R, R, True, pairs, dq_(m), k.at[m, pl.ds(0, dec_keys)],
                        tt.at[:, rows_of(m * R, R)], vtp, self_probs(m), bias.at[pl.ds(0, dec_keys)],
                        ot.at[:, rows_of(m * R, R)],
                    )

                twice(mix)
                fetch(3).wait()
                f1[...] = dxin[...].reshape(2 * R, features).astype(F32) + dot(ot[...].T, w[3])

                def norm(m):
                    shaped, factor = norm_of(f1[rows_of(m * R, R)])
                    xh1[m, 0:R] = shaped.astype(BF)
                    rr[m, 0:R, 0:1] = factor
                    h = shaped * gain(0)
                    da[m] = h
                    xh1[m, R : 2 * R] = h.astype(BF)

                twice(norm)
                fetch(12).wait()
                crossed = (dot(xh1[:, R : 2 * R].reshape(2 * R, features), w[12]) * 0.125).astype(BF)
                for m in range(2):
                    dqc_(m)[...] = crossed[m * R : (m + 1) * R]

            def self_backward(g):
                sides = jnp.concatenate([kt[m, :, R : 2 * R].T for m in range(2)], axis=0)
                f1[...] = da[...].reshape(2 * R, features) + dot_t(sides, w[12])

                def norm(m):
                    r = rows_of(m * R, R)
                    dt = norm_back(f1[r], xh1[m, 0:R].astype(F32), rr[m, 0:R, 0:1], gain(0))
                    f1[r] = dt
                    dqkv[0, r] = dt.astype(BF)

                for b in range(4):
                    fetch(b).wait()
                twice(norm)
                dqkv[0] = dot_t(dqkv[0], w[3]).astype(BF)
                finish_both(0, g)

                def unmix(m):
                    r = rows_of(m * R, R)
                    attend_back(
                        SELF_PAIRS, R, R, True, pairs, dqkv.at[0, r], dq_(m),
                        v.at[m, pl.ds(0, dec_keys)],
                        kt.at[m, :, pl.ds(0, R)], ktp, self_probs(m),
                        ot.at[:, r], dqkv.at[1, r], dqkv.at[2, r], pre_sum,
                    )

                twice(unmix)
                dqkv[0] = ot[...].T
                small_begin()
                finish_both(1, g)
                total = f1[...]
                for b in range(3):
                    total = total + dot_t(dqkv[b], w[b])
                low = total.astype(BF)
                for m in range(2):
                    dxin[m] = low[m * R : (m + 1) * R]
                    store_y(m).start()

            def middle(m):
                @pl.when(m == 0)
                def _():
                    for b in (13, 14, 15, 16, 17, *range(8 + TURNED, 8 + chunks)):
                        fetch(b).wait()
                    load_c(0).wait()
                    load_c(1).wait()

                for i in range(src_rows // PAIR):
                    memory_copy(m, i).wait_recv()

                keys = dot(rcv[m], w[13]).astype(BF)
                dqkv[1] = keys
                kct[...] = keys.T
                values = dot(rcv[m], w[14]).astype(BF)
                vc[...] = values
                tt[...] = values.T
                key = lax.broadcasted_iota(jnp.int32, (src_rows, PAIR), 0)
                bias[0:src_rows] = jnp.where(key < sl[m], 0.0, NEG)
                attend(
                    CROSS_PAIRS, R, src_rows, False, pairs, dqc_(m), dqkv.at[1], tt, None, cross_probs(),
                    bias.at[pl.ds(0, src_rows)], ot.at[:, pl.ds(0, R)],
                )
                f1[0:R] = da[m] + dot(ot[:, 0:R].T, w[15])
                yb = xh1.at[m, pl.ds(R, R)]

                def norm(r):
                    shaped, factor = norm_of(f1[r])
                    xh2[m, r] = shaped.astype(BF)
                    rr[m, r, 1:2] = factor
                    h = shaped * gain(1)
                    f1[r] = h
                    yb[r] = h.astype(BF)

                by_rows(R, norm)
                branch(DEC_CHUNKS, R, yb, slope, m)
                df = xh2.at[m, pl.ds(R, R)]

                def turn(r):
                    shaped, factor = norm_of(f1[r])
                    row = lax.broadcasted_iota(jnp.int32, (LN_ROWS, 1), 0) + r.start
                    on = jnp.where(row < tl[m], 1.0, 0.0)
                    grad = dct[m, r].astype(F32) * on
                    dct[m, r] = (shaped * gain(2) * on).astype(BF)
                    dt = norm_back(grad, shaped, factor, gain(2))
                    f1[r] = dt
                    df[r] = dt.astype(BF)

                by_rows(R, turn)
                store_d(m).start()
                branch_back_adapter(R, df, m)
                branch_back_feed(DEC_CHUNKS, R, df, slope, m, True)

                @pl.when(m == 1)
                def _():
                    back_copy(0, 0).wait_send()
                    back_copy(0, 1).wait_send()
                    for b in range(4):
                        fetch(b).start()
                    write_out(DEC_GRADS, g, lambda: xh2[:, R : 2 * R].reshape(2 * R, features), 2 * R)
                    start("B", 0, g)
                    write_in(DEC_GRADS, g, lambda r: xh1[:, R : 2 * R, r].reshape(2 * R, 2 * PAIR), 2 * R)
                    start("A", 0, g)

                def back(r):
                    dt = norm_back(f1[r], xh2[m, r].astype(F32), rr[m, r, 1:2], gain(1))
                    f1[r] = dt
                    dqkv[0, r] = dt.astype(BF)

                by_rows(R, back)
                grad_mixed = dot_t(dqkv[0, 0:R], w[15]).astype(BF)
                dqkv[0, 0:R] = grad_mixed
                attend_back(
                    CROSS_PAIRS, R, src_rows, False, pairs, dqkv.at[0, pl.ds(0, R)], dqc_(m), vc, kct, None,
                    cross_probs(), kt.at[m, :, pl.ds(R, R)], dqkv.at[1], dqkv.at[2], None,
                )

                span = features // 2
                for i in range(2):
                    part = pl.ds(i * span, span)
                    snd[:, part] = (dot_t(dqkv[1], w[13, part]) + dot_t(dqkv[2], w[14, part])).astype(BF)
                    back_copy(m, i).start()
                da[m] = f1[0:R]

            def store_d(m):
                return pltpu.make_async_copy(dct.at[m], tok.at[0, m, pl.ds(0, R)], osem.at[m])

            def store_y(m):
                return pltpu.make_async_copy(dxin.at[m], tok.at[0, m, pl.ds(R, R)], osem.at[2 + m])

            g = w.at[8]
            prefix_setup(R)
            self_forward()

            def turn_block(c, carry):
                fetch_in(c).wait()
                w[c] = w[4 + c].T
                return carry

            lax.fori_loop(0, chunks, turn_block, 0)
            for c in range(TURNED):
                fetch_out(c).wait()
                w[16 + c] = w[8 + c].T
            twice(middle)
            self_backward(g)
            small_middle()
            finish_both(2, g)
            small_late()
            for m in range(2):
                store_d(m).wait()
                store_y(m).wait()
            back_copy(1, 0).wait_send()
            back_copy(1, 1).wait_send()
            small_finish()

        @pl.when(section == 0)
        def _():
            encoder_loads()

        @pl.when(section == 1)
        def _():
            decoder_loads()

        greet()
        pl.when(section == 0)(encoder)
        pl.when(section == 1)(decoder)

    vm = pltpu.VMEM
    plane = nx * ny
    piece = small_rows * features // (16 * plane)
    smalls = 2 * (plane - 1) + nz - 1
    scratch = [
        vm((16 + TURNED, features, features), BF),
        vm((features, adapt), BF),
        vm((adapt, features), BF),
        vm((2, pairs, enc_keys, 2 * src_rows), BF),
        vm((2, enc_keys, features), BF),
        vm((2, enc_keys, features), BF),
        vm((2, features, src_rows), BF),
        vm((features, src_rows), BF),
        vm((features, src_rows), BF),
        vm((features, PRE_PAD), BF),
        vm((features, PRE_PAD), BF),
        vm((2, src_rows, features), BF),
        vm((2, src_rows, features), BF),
        vm((2, src_rows, 2), F32),
        vm((2, src_rows, adapt), BF),
        vm((2 * src_rows, adapt), BF),
        vm((2 * src_rows, adapt), BF),
        vm((src_rows, features), BF),
        vm((2, src_rows, features), BF),
        vm((src_rows, features), F32),
        vm((3, src_rows, features), BF),
        vm((nx - 1, ny * nz * ra, adapt), BF),
        vm((ny - 1, nz * ra, adapt), BF),
        vm((nz - 1, ra, adapt), BF),
        vm((ny - 1, nx * nz * ra, adapt), BF),
        vm((nx - 1, nz * ra, adapt), BF),
        vm((nz - 1, ra, adapt), BF),
        vm((2, PRE_PAD, features), F32),
        vm((enc_keys, PAIR), F32),
        vm((1, adapt), F32),
        vm((1, features), F32),
        vm((small_rows, features), BF),
        vm((plane - 1, 16, piece), BF),
        vm((16, piece), BF),
        vm((nz - 1, 16, piece), BF),
        vm((16, piece), BF),
        vm((small_rows, features), BF),
        vm((2, tgt_rows, features), BF),
        vm((2, tgt_rows, features), BF),
        vm((2, tgt_rows, features), F32),
        vm((src_rows, features), BF),
        vm((features, src_rows), BF),
        pltpu.SemaphoreType.DMA((18,)),
        pltpu.SemaphoreType.DMA((4,)),
        pltpu.SemaphoreType.DMA((4,)),
        pltpu.SemaphoreType.DMA((4,)),
        pltpu.SemaphoreType.DMA((4,)),
        pltpu.SemaphoreType.DMA((18,)),
        pltpu.SemaphoreType.DMA((18,)),
        pltpu.SemaphoreType.DMA((smalls,)),
        pltpu.SemaphoreType.DMA((smalls,)),
    ]
    return kernel, scratch, ra


def finish(tok, ig_in, og_in, small_in, tok_out, pre_out, ig_out, og_out, ib_out, ob_out, held, ig, og, small, sem):
    micro = tok.shape[1]
    loads = [pltpu.make_async_copy(tok.at[0, m], held.at[0, m], sem.at[m]) for m in range(micro)]
    stores = [pltpu.make_async_copy(held.at[0, m], tok_out.at[0, m], sem.at[micro + m]) for m in range(micro)]
    rest = [(small_in, small, 4), (ig_in, ig, 5), (og_in, og, 6)]
    rest = [pltpu.make_async_copy(a, b, sem.at[i]) for a, b, i in rest]
    for copy in loads + rest:
        copy.start()
    for load, store in zip(loads, stores):
        load.wait()
        store.start()
    for copy in rest:
        copy.wait()
    adapt = ig.shape[1]
    pre_out[:, 0, :] = small[0:PRE]
    pre_out[:, 1, :] = small[PRE_PAD : PRE_PAD + PRE]
    ig_out[0] = ig[...]
    og_out[0] = og[...]
    ob_out[...] = small[PRE : PRE + 1]
    ib_out[...] = small[PRE_PAD + PRE : PRE_PAD + PRE + 1, 0:adapt]
    for store in stores:
        store.wait()


def solution(mesh):
    dp = mesh.shape["dp"]
    nz = 4
    nx = math.isqrt(dp // nz)
    ny = dp // (nz * nx)

    def per_device(
        source, target, cotangent, source_lengths, target_lengths, attention_in, attention_out,
        cross_query, cross_pair, cross_output, feed_in, feed_out, adapter_in, adapter_in_bias,
        adapter_out, adapter_out_bias, prefix, norm_gains,
    ):
        features = source.shape[2]
        adapt = adapter_in.shape[2]
        kernel, scratch, ra = make_kernel(
            nz, ny, nx, features, feed_in.shape[2], adapt, source.shape[1], target.shape[1]
        )
        anywhere = pl.BlockSpec(memory_space=pl.ANY)
        scalar = pl.BlockSpec(memory_space=pltpu.SMEM)
        vector = pl.BlockSpec(memory_space=pltpu.VMEM)
        tok, ig, og, small = pl.pallas_call(
            kernel,
            out_shape=(
                jax.ShapeDtypeStruct((1, source.shape[0], source.shape[1], features), BF),
                jax.ShapeDtypeStruct((ra, adapt), F32),
                jax.ShapeDtypeStruct((ra // 2, features), F32),
                jax.ShapeDtypeStruct((2 * PRE_PAD, features), F32),
            ),
            in_specs=[anywhere] * 3 + [scalar] * 2 + [anywhere] * 9 + [vector] * 4,
            out_specs=(anywhere, vector, vector, vector),
            scratch_shapes=scratch,
            compiler_params=pltpu.CompilerParams(
                collective_id=0, has_side_effects=True, vmem_limit_bytes=67000000
            ),
        )(
            source, target, cotangent, source_lengths.reshape(-1), target_lengths.reshape(-1), attention_in,
            attention_out, cross_query, cross_pair, cross_output, feed_in, feed_out, adapter_in, adapter_out,
            adapter_in_bias, adapter_out_bias, prefix[0].transpose(1, 0, 2), norm_gains,
        )
        tok, pre, ig, og, ib, ob = pl.pallas_call(
            finish,
            out_shape=(
                jax.ShapeDtypeStruct(tok.shape, BF),
                jax.ShapeDtypeStruct((PRE, 2, features), F32),
                jax.ShapeDtypeStruct((1, ra, adapt), F32),
                jax.ShapeDtypeStruct((1, ra // 2, features), F32),
                jax.ShapeDtypeStruct((1, adapt), F32),
                jax.ShapeDtypeStruct((1, features), F32),
            ),
            in_specs=[anywhere, anywhere, anywhere, anywhere],
            out_specs=(anywhere, vector, vector, vector, vector, vector),
            scratch_shapes=[
                pltpu.VMEM(tok.shape, BF),
                pltpu.VMEM(ig.shape, F32),
                pltpu.VMEM(og.shape, F32),
                pltpu.VMEM(small.shape, F32),
                pltpu.SemaphoreType.DMA((7,)),
            ],
        )(tok, ig, og, small)
        return tok, pre.transpose(1, 0, 2)[None], ig, og, ib, ob

    return jax.shard_map(
        per_device,
        mesh=mesh,
        in_specs=(
            P(None, "dp", None),
            P(None, "dp", None),
            P(None, "dp", None),
            P(None, "dp"),
            P(None, "dp"),
            P("section", None, None),
            P("section", None, None),
            P(),
            P(),
            P(),
            P("section", None, None),
            P("section", None, None),
            P("section", None, None),
            P("section", None),
            P("section", None, None),
            P("section", None),
            P("section", None, None, None),
            P("section", None, None),
        ),
        out_specs=(
            P("section", None, "dp", None),
            P("section", None, None, None),
            P("section", "dp", None),
            P("section", "dp", None),
            P("section", None),
            P("section", None),
        ),
        check_vma=False,
    )
```
